32 devices in a mesh: groups: 2 (over y), req: 4 (over x, core), tp: 4 (over z).
Axes of the slice: x: 2, y: 2, z: 4, core: 2. Of those that a mesh axis runs over, the one named last changes fastest.
Arguments:
- x_in: bfloat16 [8192, 16384], P(('groups', 'req'), 'tp'), parts along dimension 0, may hold values from -6 to 6
- gate_in: bfloat16 [8192, 16384], P(('groups', 'req'), 'tp'), parts along dimension 0, may hold values from -6 to 6
- b_in: bfloat16 [8192, 2048], P(('groups', 'req'), 'tp'), parts along dimension 0, may hold values from -6 to 6
- c_in: bfloat16 [8192, 2048], P(('groups', 'req'), 'tp'), parts along dimension 0, may hold values from -6 to 6
- dt_raw: bfloat16 [8192, 256], P(('groups', 'req'), 'tp'), parts along dimension 0, may hold values from -3 to 3
- conv_x: bfloat16 [4, 16384], P(None, 'tp'), may hold values from -3 to 3
- conv_b: bfloat16 [4, 2048], P(None, 'tp'), may hold values from -3 to 3
- conv_c: bfloat16 [4, 2048], P(None, 'tp'), may hold values from -3 to 3
- dt_bias: float32 [256], P('tp'), may hold values from -3 to 0
- a_log: float32 [256], P('tp'), may hold values from -7 to -2.5
- skip: float32 [256], P('tp'), may hold values from 0.5 to 1.5
- norm_gain: float32 [16384], P('tp'), may hold values from 0.5 to 1.5
- segment: int32 [8192], P(('groups', 'req')), parts along dimension 0, may hold values from 0 to 3, never falling along the last dimension, each value on 1 to 2048 neighbouring positions
Outputs:
- mixed: bfloat16 [8192, 16384], P(('groups', 'req'), 'tp'), parts along dimension 0
The draws below stay inside these ranges and needn't reach their ends.
There are 2 independent parts, one for each index of `groups`. The reference program is written for one: setup_inputs(seed, part) draws one part's arguments, and reference() takes and returns one part's arrays. A program takes and returns all parts, laid end to end along the dimension named above; an argument that names none is the same for every part. Nothing has to cross between parts.
Inputs may be any that keep to these rules, and one draw needn't show every extreme that they name: `segment`: never falls along the stream; each prompt's tokens are contiguous; one prompt has exactly 2048 tokens.
All inputs are finite; a program needn't handle non-finite values.
Results may differ from the reference program's by a relative error of at most 0.0085.
Values may be sent and summed in bfloat16 or wider, within the bound.
No kernel may reach another device: no remote copies, remote signals or barrier semaphores. Data moves between devices by JAX's collectives and lax.ppermute only.
A program may use at most 256 MiB of HBM per device.

```python
import math
import jax
import jax.numpy as jnp
import numpy as np
from jax import lax

H = 256
P_SIZE = 64
N = 256
G = 8
L = 256
KCONV = 4
TOKENS = 4096


def block_levels(key, dims, cuts, smallest, largest):
    def one(axis_at, blocks):
        heights = jax.random.uniform(jax.random.fold_in(jax.random.fold_in(key, 6), axis_at), (blocks,), jnp.float32, smallest / len(cuts), largest / len(cuts))
        return jnp.repeat(jnp.exp(heights), dims[axis_at] // blocks).reshape((-1,) + (1,) * (len(dims) - axis_at - 1))

    level = one(*cuts[0])
    for cut in cuts[1:]:
        level = level * one(*cut)
    return level


def split_up(count, total, bound, lean):
    loads = [(1 << 20) // math.isqrt(rank ** lean) + 1 for rank in range(2, count + 1)]
    surplus, given = total - bound - (count - 1), [1] * (count - 1)
    while surplus > 0:
        free = [i for i in range(count - 1) if given[i] < bound]
        mass, left = sum([loads[i] for i in free]), surplus
        for i in free:
            extra = min(bound - given[i], max(1, left * loads[i] // mass), surplus)
            given[i] = given[i] + extra
            surplus = surplus - extra
    return np.array([bound] + given)


def ragged(rng, number_of, total, limit, skew):
    if number_of == 2:
        one = jax.random.randint(rng, (), max(1, total - limit), min(limit, total - 1) + 1)
        return jnp.stack([one, total - one])
    lengths = jnp.asarray(split_up(number_of, total, limit, skew), jnp.int32)
    couples = (number_of - 1) // 2
    giver, taker = lengths[1:1 + 2 * couples:2], lengths[2:2 + 2 * couples:2]
    room = jnp.minimum(giver - 1, limit - taker)
    passed = jax.random.randint(jax.random.fold_in(rng, 1), (couples,), 0, 1 << 20) % (room + 1)
    lengths = lengths.at[1:1 + 2 * couples:2].set(giver - passed).at[2:2 + 2 * couples:2].set(taker + passed)
    return lengths[jax.random.permutation(jax.random.fold_in(rng, 2), number_of)]


def scatter_about(own_key, shape, width, limit, shards=(), held_as=jnp.bfloat16):
    values = width * jax.random.normal(own_key, shape, jnp.float32)
    if shards:
        values = values * block_levels(own_key, shape, shards, -0.22, 0.18)
    return jnp.clip(values, -limit, limit).astype(held_as)


def setup_inputs(seed: int = 0, part: int = 0) -> dict:
    key_list = jax.random.split(jax.random.key(seed), 14)
    own_keys = jax.random.split(jax.random.fold_in(key_list[13], part), 14)
    return {
        "x_in": scatter_about(own_keys[0], (TOKENS, H * P_SIZE), 1.0, 6.0, ((0, 4), (1, 4))),
        "gate_in": scatter_about(own_keys[1], (TOKENS, H * P_SIZE), 1.0, 6.0, ((0, 4), (1, 4))),
        "b_in": scatter_about(own_keys[2], (TOKENS, G * N), 1.0, 6.0, ((0, 4), (1, 4))),
        "c_in": scatter_about(own_keys[3], (TOKENS, G * N), 1.0, 6.0, ((0, 4), (1, 4))),
        "dt_raw": scatter_about(own_keys[4], (TOKENS, H), 0.5, 3.0, ((0, 4), (1, 4))),
        "conv_x": scatter_about(key_list[5], (KCONV, H * P_SIZE), KCONV ** -0.5, 3.0, ((1, 4),)),
        "conv_b": scatter_about(key_list[6], (KCONV, G * N), KCONV ** -0.5, 3.0, ((1, 4),)),
        "conv_c": scatter_about(key_list[7], (KCONV, G * N), KCONV ** -0.5, 3.0, ((1, 4),)),
        "dt_bias": jnp.clip(-3.0 + 3.0 * jax.random.uniform(key_list[8], (H,), jnp.float32) ** block_levels(key_list[8], (H,), ((0, 4),), -0.2, 0.2), -3.0, 0.0),
        "a_log": jnp.clip(-7.0 + 4.5 * jax.random.uniform(key_list[9], (H,), jnp.float32) ** block_levels(key_list[9], (H,), ((0, 4),), -0.2, 0.2), -7.0, -2.5),
        "skip": jnp.clip(0.5 + 1.0 * jax.random.uniform(key_list[10], (H,), jnp.float32) ** block_levels(key_list[10], (H,), ((0, 4),), -0.2, 0.2), 0.5, 1.5),
        "norm_gain": jnp.clip(0.5 + 1.0 * jax.random.uniform(key_list[11], (H * P_SIZE,), jnp.float32) ** block_levels(key_list[11], (H * P_SIZE,), ((0, 4),), -0.2, 0.2), 0.5, 1.5),
        "segment": jnp.searchsorted(jnp.cumsum(ragged(own_keys[12], 4, TOKENS, TOKENS // 2, 2)), jnp.arange(TOKENS), side="right").astype(jnp.int32),
    }


def causal_conv(window, weight, seg_window):
    length = window.shape[0] - KCONV + 1
    own = seg_window[KCONV - 1:]
    acc = jnp.zeros((length, window.shape[1]), jnp.float32)
    for tap in range(KCONV):
        rows = lax.slice_in_dim(window, tap, tap + length, axis=0).astype(jnp.float32)
        same = (lax.slice_in_dim(seg_window, tap, tap + length) == own)[:, None]
        acc = acc + jnp.where(same, rows * weight[tap].astype(jnp.float32), 0.0)
    return jax.nn.silu(acc).astype(jnp.bfloat16)

def block_terms(xs, bs, cs, dt, seg, before, rate):
    length = seg.shape[0]
    cum = jnp.cumsum(-dt * rate, axis=0)
    cum_heads = jnp.transpose(cum, (1, 2, 0))
    spots = jnp.arange(length, dtype=jnp.int32)
    allowed = (seg[:, None] == seg[None, :]) & (spots[:, None] >= spots[None, :])
    decay = jnp.exp(jnp.where(allowed, cum_heads[..., :, None] - cum_heads[..., None, :], -jnp.inf))
    scores = jnp.einsum('ign,jgn->gij', cs.astype(jnp.float32), bs.astype(jnp.float32))
    dt_heads = jnp.transpose(dt, (1, 2, 0))
    weights = (scores[:, None] * decay * dt_heads[..., None, :]).astype(jnp.bfloat16)
    intra = jnp.einsum('gkij,jgkp->igkp', weights.astype(jnp.float32), xs.astype(jnp.float32))
    latest = (seg == seg[-1])[:, None, None]
    tail_weight = jnp.where(latest, jnp.exp(cum[-1] - cum), 0.0) * dt
    scaled_b = (bs[:, :, None, :].astype(jnp.float32) * tail_weight[..., None]).astype(jnp.bfloat16)
    state = jnp.einsum('jgkn,jgkp->gknp', scaled_b.astype(jnp.float32), xs.astype(jnp.float32))
    passes = jnp.all(seg == before)
    factor = jnp.where(passes, jnp.exp(cum[-1]), 0.0)
    enter = jnp.where((seg == before)[:, None, None], jnp.exp(cum), 0.0)
    return (intra, state, factor, enter)

def gated_norm(values, gate, gain, parts):
    mixed = values.astype(jnp.float32) * jax.nn.silu(gate.astype(jnp.float32))
    count = mixed.shape[0]
    mixed = mixed.reshape(count, parts, -1)
    scale = lax.rsqrt(lax.optimization_barrier(jnp.mean(mixed * mixed, axis=-1, keepdims=True)) + 1e-05)
    return ((mixed * scale).reshape(count, -1) * gain).astype(jnp.bfloat16)

def reference(x_in, gate_in, b_in, c_in, dt_raw, conv_x, conv_b, conv_c, dt_bias, a_log, skip, norm_gain, segment):
    total = x_in.shape[0]
    count = total // L
    reach = KCONV - 1
    per_group = H // G

    def padded(values):
        return jnp.concatenate([jnp.zeros((reach, values.shape[1]), values.dtype), values], axis=0)
    x_pad = padded(x_in)
    b_pad = padded(b_in)
    c_pad = padded(c_in)
    seg_pad = jnp.concatenate([jnp.full((reach,), -1, jnp.int32), segment.astype(jnp.int32)])
    rate = jnp.exp(a_log).reshape(G, per_group)
    skip_heads = skip.reshape(G, per_group)[:, :, None]

    def step(carry, index):
        start = (index * L).astype(jnp.int32)
        seg_window = lax.dynamic_slice_in_dim(seg_pad, start, L + reach)
        xs = causal_conv(lax.dynamic_slice_in_dim(x_pad, start, L + reach, 0), conv_x, seg_window)
        bs = causal_conv(lax.dynamic_slice_in_dim(b_pad, start, L + reach, 0), conv_b, seg_window)
        cs = causal_conv(lax.dynamic_slice_in_dim(c_pad, start, L + reach, 0), conv_c, seg_window)
        raw = lax.dynamic_slice_in_dim(dt_raw, start, L, 0).astype(jnp.float32)
        dt = jax.nn.softplus(raw + dt_bias).reshape(L, G, per_group)
        seg = seg_window[reach:]
        before = seg_window[reach - 1]
        xs_heads = xs.reshape(L, G, per_group, P_SIZE)
        cs_groups = cs.reshape(L, G, N)
        intra, state, factor, enter = block_terms(xs_heads, bs.reshape(L, G, N), cs_groups, dt, seg, before, rate)
        inter = enter[..., None] * jnp.einsum('ign,gknp->igkp', cs_groups.astype(jnp.float32), carry, precision=lax.Precision.HIGHEST)
        total_y = intra + inter + skip_heads * xs_heads.astype(jnp.float32)
        y = total_y.astype(jnp.bfloat16).reshape(L, H * P_SIZE)
        gate = lax.dynamic_slice_in_dim(gate_in, start, L, 0)
        out = gated_norm(y, gate, norm_gain, G)
        new = factor[..., None, None] * carry + state
        return (new, out)
    init = jnp.zeros((G, per_group, N, P_SIZE), jnp.float32)
    _, outs = lax.scan(step, init, jnp.arange(count, dtype=jnp.int32))
    return outs.reshape(total, H * P_SIZE)
```

```python
import functools

import jax
import jax.numpy as jnp
from jax import lax
from jax.experimental import pallas as pl
from jax.experimental.pallas import tpu as pltpu
from jax.sharding import PartitionSpec as P

P_SIZE = 64
N = 256
L = 256
KCONV = 4
REACH = KCONV - 1
LANES = 128
CHUNK = 256
F32 = jnp.float32
BF16 = jnp.bfloat16


def dot(a, b):
    return jnp.dot(a, b, preferred_element_type=F32)


def split_high_low(value, heads):
    lane = lax.broadcasted_iota(jnp.int32, value.shape, 1)
    high = value.astype(BF16).astype(F32)
    low = jnp.where(lane < 2 * heads, value - high, 0.0)
    return jnp.where(lane < heads, high, low).astype(BF16)


def silu_of_half(half):
    return half + half * jnp.tanh(half)


def conv_tile(buf, index, weights, lanes, row, rows, code):
    acc = None
    for step in range(KCONV):
        term = buf[index, pl.ds(8 - step + row, rows), :] * weights[REACH - step : KCONV - step, lanes]
        if code is not None and step > 0:
            term = jnp.where(code >= step, term, 0.0)
        acc = term if acc is None else acc + term
    return acc


def prep_kernel(
    seg_s, halo_s, b_ref, c_ref, halo_ref, wb_ref, wc_ref, dt_ref, bias_ref, rate_ref, seg_ref,
    mb_ref, cm_ref, ci_ref, a_ref, e_ref, q_ref, em_ref, code_ref,
    bc_buf, seg_buf, off_ref, *, parts
):
    block = pl.program_id(0)
    width = parts * N
    pieces = width // LANES
    before_device = halo_s[REACH - 1]
    before = jnp.where(block == 0, before_device, seg_s[jnp.maximum(block * L - 1, 0)])
    last = seg_s[block * L + L - 1]

    @pl.when(block == 0)
    def _():
        off_ref[...] = jnp.zeros_like(off_ref)
        for k in range(REACH):
            seg_buf[pl.ds(8 - REACH + k, 1), :] = jnp.full((1, LANES), halo_s[k], jnp.int32).astype(F32)
        for piece in range(2 * pieces):
            bc_buf[piece, pl.ds(8 - REACH, REACH), :] = halo_ref[:, piece * LANES : (piece + 1) * LANES].astype(F32)

    @pl.when(block > 0)
    def _():
        seg_buf[0:8, :] = seg_buf[L : L + 8, :]
        for piece in range(2 * pieces):
            bc_buf[piece, 0:8, :] = bc_buf[piece, L : L + 8, :]

    seg_row = seg_ref[pl.ds(block, 1), :].astype(F32)
    seg_col = jnp.transpose(jnp.broadcast_to(seg_row, (L, L)))
    seg_buf[8 : 8 + L, :] = seg_col[:, :LANES]
    own = seg_col[:, :LANES]
    code = jnp.zeros((L, LANES), F32)
    for step in range(1, KCONV):
        code = code + jnp.where(seg_buf[pl.ds(8 - step, L), :] == own, 1.0, 0.0)
    code_ref[...] = code

    for piece in range(pieces):
        lanes = slice(piece * LANES, (piece + 1) * LANES)
        bc_buf[piece, 8 : 8 + L, :] = b_ref[:, lanes].astype(F32)
        bc_buf[pieces + piece, 8 : 8 + L, :] = c_ref[:, lanes].astype(F32)

    def conved(first, w_ref):
        cols = []
        for piece in range(N // LANES):
            index = first * (N // LANES) + piece
            inner = index % pieces
            lanes = slice(inner * LANES, (inner + 1) * LANES)
            acc = conv_tile(bc_buf, index, w_ref, lanes, 0, L, code)
            cols.append(silu_of_half(acc))
        return jnp.concatenate(cols, axis=1)

    spot_row = lax.broadcasted_iota(jnp.int32, (L, L), 0)
    spot_col = lax.broadcasted_iota(jnp.int32, (L, L), 1)
    causal = spot_row >= spot_col
    allowed = causal & (seg_col == seg_row)
    latest = seg_col == last.astype(F32)
    enters = seg_col == before.astype(F32)
    enters_device = seg_col == before_device.astype(F32)
    for g in range(parts):
        bs = conved(g, wb_ref)
        cs = conved(parts + g, wc_ref)
        scores = lax.dot_general(
            cs.astype(BF16), bs.astype(BF16), (((1,), (1,)), ((), ())), preferred_element_type=F32
        )
        mb_ref[g, 0, 0:L, :] = jnp.where(allowed, scores, 0.0).astype(BF16)
        mb_ref[g, 0, L : L + N, :] = jnp.transpose(jnp.where(latest, bs, 0.0)).astype(BF16)
        cols = slice(g * N, (g + 1) * N)
        cm_ref[:, cols] = jnp.where(enters, cs, 0.0).astype(BF16)
        ci_ref[:, cols] = jnp.where(enters_device, cs, 0.0).astype(BF16)

    raw = dt_ref[...].astype(F32)
    heads = raw.shape[1]
    z = jnp.concatenate([raw] * (LANES // heads), axis=1) + bias_ref[...]
    dt = jnp.maximum(z, 0.0) + jnp.log1p(jnp.exp(-jnp.abs(z)))
    cum = jnp.dot(
        jnp.where(causal, 1.0, 0.0), -dt * rate_ref[...], precision=lax.Precision.HIGHEST, preferred_element_type=F32
    )
    total = cum[L - 1 : L, :]
    middle = 0.5 * total
    a_ref[...] = split_high_low(jnp.exp(middle - cum) * dt, heads)
    e_ref[...] = split_high_low(jnp.exp(cum - middle), heads)
    q_ref[...] = split_high_low(jnp.exp(cum + off_ref[0:1, :]), heads)
    em_ref[0] = split_high_low(jnp.broadcast_to(jnp.exp(middle), (16, LANES)), heads)
    off_ref[...] = off_ref[...] + total


def spread_matrix(ref, first_head, heads):
    width = ref.shape[1]
    rows = lax.broadcasted_iota(jnp.int32, (LANES, width), 0) % heads
    cols = lax.broadcasted_iota(jnp.int32, (LANES, width), 1) // P_SIZE
    ref[...] = jnp.where(rows == cols + first_head, 1.0, 0.0).astype(BF16)


def local_kernel(
    seg_s, halo_s, x_ref, halo_ref, w_ref, skip_ref, mb_ref, cm_ref, a_ref, e_ref, em_ref, code_ref,
    y_ref, state_ref, factor_ref,
    buf, carry, spread, *, first_head, heads, blocks
):
    block = pl.program_id(0)
    width = x_ref.shape[1]
    chunks = width // CHUNK
    inner = CHUNK // LANES
    start = block * L
    last = seg_s[start + L - 1]
    first = seg_s[start]
    before_device = halo_s[REACH - 1]
    before = jnp.where(block == 0, before_device, seg_s[jnp.maximum(start - 1, 0)])
    oldest = jnp.where(block == 0, halo_s[0], seg_s[jnp.maximum(start - REACH, 0)])
    cut = (first != last) | ((oldest != first) & (oldest >= 0))
    passes = jnp.where(before == last, 1.0, 0.0)

    @pl.when(block == 0)
    def _():
        spread_matrix(spread, first_head, heads)
        carry[...] = jnp.zeros_like(carry)
        factor_ref[...] = jnp.ones_like(factor_ref)
        for piece in range(width // LANES):
            buf[piece, pl.ds(8 - REACH, REACH), :] = halo_ref[:, piece * LANES : (piece + 1) * LANES].astype(F32)

    @pl.when(block > 0)
    def _():
        buf[:, 0:8, :] = buf[:, L : L + 8, :]

    def body(masked, chunk, _):
        base = pl.multiple_of(chunk * CHUNK, CHUNK)
        cols = pl.ds(base, CHUNK)
        part = spread[:, cols]
        scale = dot(a_ref[...], part)
        xs_cols, u_cols = [], []
        for piece in range(inner):
            index = chunk * inner + piece
            lanes = pl.ds(pl.multiple_of(base + piece * LANES, LANES), LANES)
            buf[index, 8 : 8 + L, :] = x_ref[:, lanes].astype(F32)
            code = code_ref[...] if masked else None
            acc = conv_tile(buf, index, w_ref, lanes, 0, L, code)
            xs = silu_of_half(acc)
            xs_cols.append(xs)
            u_cols.append((xs * scale[:, piece * LANES : (piece + 1) * LANES]).astype(BF16))
        u = jnp.concatenate(u_cols, axis=1)
        half = dot(em_ref[0], part)[0:1, :]
        old = carry[:, cols] * half
        both = dot(mb_ref[0, 0], u)
        grown = dot(cm_ref[...], old.astype(BF16))
        out = dot(e_ref[...], part) * (both[0:L] + grown)
        xs = jnp.concatenate(xs_cols, axis=1)
        y_ref[:, cols] = (out + skip_ref[:, cols] * xs).astype(BF16)
        new = half * (passes * old + both[L : L + N])
        carry[:, cols] = new
        factor_ref[:, cols] = factor_ref[:, cols] * (passes * half * half)

        @pl.when(block == blocks - 1)
        def _():
            state_ref[:, cols] = new.astype(BF16)

        return 0

    @pl.when(cut)
    def _():
        lax.fori_loop(0, chunks, functools.partial(body, True), 0)

    @pl.when(jnp.logical_not(cut))
    def _():
        lax.fori_loop(0, chunks, functools.partial(body, False), 0)


def final_kernel(
    y_ref, gate_ref, ci_ref, q_ref, t0_ref, t1_ref, t2_ref, gain_ref, out_ref,
    total, spread, held, *, first_head, heads
):
    width = y_ref.shape[1]
    chunks = width // CHUNK

    @pl.when(pl.program_id(0) == 0)
    def _():
        spread_matrix(spread, first_head, heads)
        total[...] = (t0_ref[...].astype(F32) + t1_ref[...].astype(F32) + t2_ref[...].astype(F32)).astype(BF16)

    def body(chunk, squares):
        cols = pl.ds(pl.multiple_of(chunk * CHUNK, CHUNK), CHUNK)
        come = dot(ci_ref[...], total[:, cols]) * dot(q_ref[...], spread[:, cols])
        half = 0.5 * gate_ref[:, cols].astype(F32)
        v = (y_ref[:, cols].astype(F32) + come) * silu_of_half(half)
        held[:, cols] = v
        v2 = v * v
        for piece in range(CHUNK // LANES):
            squares = squares + v2[:, piece * LANES : (piece + 1) * LANES]
        return squares

    squares = lax.fori_loop(0, chunks, body, jnp.zeros((L, LANES), F32))
    mean = jnp.sum(squares, axis=1, keepdims=True) * (1.0 / width)
    scale = lax.rsqrt(mean + 1e-05)

    def close(chunk, _):
        cols = pl.ds(pl.multiple_of(chunk * CHUNK, CHUNK), CHUNK)
        out_ref[:, cols] = (held[:, cols] * scale * gain_ref[:, cols]).astype(BF16)
        return 0

    lax.fori_loop(0, chunks, close, 0)


def final_into_kernel(*refs, first_head, heads):
    final_kernel(*refs[:8], *refs[9:], first_head=first_head, heads=heads)


def per_device(
    x_in, gate_in, b_in, c_in, dt_raw, conv_x, conv_b, conv_c, dt_bias, a_log, skip, norm_gain, segment
):
    rows, channels = x_in.shape
    width_bc = b_in.shape[1]
    parts = width_bc // N
    width = channels // parts
    heads = width // P_SIZE
    all_heads = dt_raw.shape[1]
    blocks = rows // L
    devices = lax.axis_size("req")
    params = functools.partial(pltpu.CompilerParams, dimension_semantics=("arbitrary",))
    shape = jax.ShapeDtypeStruct

    shift = [(k, k + 1) for k in range(devices - 1)]
    inside = [(k, k + 1) for k in range(0, devices - 1, 2)]
    across = [(k, k + 1) for k in range(1, devices - 1, 2)]
    tail = jnp.concatenate([x_in[rows - REACH :], b_in[rows - REACH :], c_in[rows - REACH :]], axis=1)
    halo = lax.ppermute(tail, "req", shift)
    halo_ids = lax.ppermute(segment[rows - REACH :] + 1, "req", shift) - 1

    repeated = lambda value: jnp.tile(value, LANES // all_heads).reshape(1, -1)
    half_x, half_b, half_c = (0.5 * weight.astype(F32) for weight in (conv_x, conv_b, conv_c))
    whole = lambda *_: (0, 0)
    at_block = lambda block, *_: (block, 0)
    narrow = pl.BlockSpec((L, LANES), at_block)
    small = shape((rows, LANES), BF16)
    mb, cm, ci, a_hl, e_hl, q_hl, em, code = pl.pallas_call(
        functools.partial(prep_kernel, parts=parts),
        grid_spec=pltpu.PrefetchScalarGridSpec(
            num_scalar_prefetch=2,
            grid=(blocks,),
            in_specs=[
                pl.BlockSpec((L, width_bc), at_block),
                pl.BlockSpec((L, width_bc), at_block),
                pl.BlockSpec((REACH, 2 * width_bc), lambda *_: (0, channels // (2 * width_bc))),
                pl.BlockSpec((KCONV, width_bc), whole),
                pl.BlockSpec((KCONV, width_bc), whole),
                pl.BlockSpec((L, all_heads), at_block),
                pl.BlockSpec((1, LANES), whole),
                pl.BlockSpec((1, LANES), whole),
                pl.BlockSpec((blocks, L), whole),
            ],
            out_specs=[
                pl.BlockSpec((parts, 1, L + N, L), lambda block, *_: (0, block, 0, 0)),
                pl.BlockSpec((L, width_bc), at_block),
                pl.BlockSpec((L, width_bc), at_block),
                narrow,
                narrow,
                narrow,
                pl.BlockSpec((1, 16, LANES), lambda block, *_: (block, 0, 0)),
                narrow,
            ],
            scratch_shapes=[
                pltpu.VMEM((2 * width_bc // LANES, L + 8, LANES), F32),
                pltpu.VMEM((L + 8, LANES), F32),
                pltpu.VMEM((8, LANES), F32),
            ],
        ),
        out_shape=[
            shape((parts, blocks, L + N, L), BF16),
            shape((rows, width_bc), BF16),
            shape((rows, width_bc), BF16),
            small,
            small,
            small,
            shape((blocks, 16, LANES), BF16),
            shape((rows, LANES), F32),
        ],
        compiler_params=params(vmem_limit_bytes=24 << 20),
        cost_estimate=pl.CostEstimate(flops=10**9, bytes_accessed=6 << 20, transcendentals=0),
        name="prep",
    )(
        segment, halo_ids, b_in, c_in, halo, half_b, half_c, dt_raw,
        repeated(dt_bias), repeated(jnp.exp(a_log)), segment.reshape(blocks, L),
    )

    skip_row = jnp.repeat(skip, P_SIZE).reshape(1, -1)
    gain_row = norm_gain.reshape(1, -1)

    def local(g):
        at_group = lambda *_: (0, g)
        return pl.pallas_call(
            functools.partial(local_kernel, first_head=g * heads, heads=all_heads, blocks=blocks),
            grid_spec=pltpu.PrefetchScalarGridSpec(
                num_scalar_prefetch=2,
                grid=(blocks,),
                in_specs=[
                    pl.BlockSpec((L, width), lambda block, *_: (block, g)),
                    pl.BlockSpec((REACH, width), at_group),
                    pl.BlockSpec((KCONV, width), at_group),
                    pl.BlockSpec((1, width), at_group),
                    pl.BlockSpec((1, 1, L + N, L), lambda block, *_: (g, block, 0, 0)),
                    pl.BlockSpec((L, N), lambda block, *_: (block, g)),
                    narrow,
                    narrow,
                    pl.BlockSpec((1, 16, LANES), lambda block, *_: (block, 0, 0)),
                    narrow,
                ],
                out_specs=[
                    pl.BlockSpec((L, width), at_block),
                    pl.BlockSpec((N, width), whole),
                    pl.BlockSpec((1, width), whole),
                ],
                scratch_shapes=[
                    pltpu.VMEM((width // LANES, L + 8, LANES), F32),
                    pltpu.VMEM((N, width), F32),
                    pltpu.VMEM((LANES, width), BF16),
                ],
            ),
            out_shape=[shape((rows, width), BF16), shape((N, width), BF16), shape((1, width), F32)],
            compiler_params=params(vmem_limit_bytes=24 << 20),
            cost_estimate=pl.CostEstimate(flops=6 * 10**9, bytes_accessed=16 << 20, transcendentals=0),
            name="local",
        )(segment, halo_ids, x_in, halo, half_x, skip_row, mb, cm, a_hl, e_hl, em, code)

    def travel(state, factor):
        def scaled(value):
            return factor * value.astype(F32)

        first = lax.ppermute(state, "req", inside)
        leaving = (state.astype(F32) + scaled(first)).astype(BF16)
        entering, passed = jnp.zeros_like(state), jnp.zeros_like(state)
        rounds = devices // 2 - 1
        for turn in range(rounds):
            entering = lax.ppermute(leaving, "req", across)
            passed = lax.ppermute(scaled(entering).astype(BF16), "req", inside)
            if turn < rounds - 1:
                leaving = (state.astype(F32) + scaled(first.astype(F32) + passed.astype(F32))).astype(BF16)
        return first, entering, passed

    def final(g, y, carries, out):
        at_group = lambda *_: (0, g)
        own = pl.BlockSpec((L, width), lambda block: (block, g))
        in_specs = [
            pl.BlockSpec((L, width), at_block),
            own,
            pl.BlockSpec((L, N), lambda block: (block, g)),
            narrow,
            pl.BlockSpec((N, width), whole),
            pl.BlockSpec((N, width), whole),
            pl.BlockSpec((N, width), whole),
            pl.BlockSpec((1, width), at_group),
        ]
        operands = [y, gate_in, ci, q_hl, *carries, gain_row]
        if out is not None:
            in_specs.append(pl.BlockSpec(memory_space=pl.ANY))
            operands.append(out)
        return pl.pallas_call(
            functools.partial(final_kernel if out is None else final_into_kernel, first_head=g * heads, heads=all_heads),
            grid=(blocks,),
            in_specs=in_specs,
            out_specs=own,
            out_shape=shape((rows, channels), BF16),
            scratch_shapes=[
                pltpu.VMEM((N, width), BF16),
                pltpu.VMEM((LANES, width), BF16),
                pltpu.VMEM((L, width), F32),
            ],
            input_output_aliases={} if out is None else {8: 0},
            compiler_params=params(vmem_limit_bytes=24 << 20),
            cost_estimate=pl.CostEstimate(flops=4 * 10**9, bytes_accessed=16 << 20, transcendentals=0),
            name="final",
        )(*operands)

    locals_ = [local(g) for g in range(parts)]
    carries = [travel(state, factor) for _, state, factor in locals_]
    out = None
    for g in range(parts):
        out = final(g, locals_[g][0], carries[g], out)
    return out


def solution(mesh):
    rows = P(("groups", "req"), "tp")
    placed = (rows,) * 5 + (P(None, "tp"),) * 3 + (P("tp"),) * 4 + (P(("groups", "req")),)
    return jax.shard_map(
        per_device,
        mesh=mesh,
        in_specs=placed,
        out_specs=rows,
        check_vma=False,
    )
```

```python
import functools

import jax
import jax.numpy as jnp
from jax import lax
from jax.experimental import pallas as pl
from jax.experimental.pallas import tpu as pltpu
from jax.sharding import PartitionSpec as P

P_SIZE = 64
N = 256
L = 256
SPAN = 2 * L
KCONV = 4
REACH = KCONV - 1
LANES = 128
CHUNK = 256
TILE = 128
F32 = jnp.float32
BF16 = jnp.bfloat16


def dot(a, b):
    return jnp.dot(a, b, preferred_element_type=F32)


def split_high_low(value, heads):
    lane = lax.broadcasted_iota(jnp.int32, value.shape, 1)
    high = value.astype(BF16).astype(F32)
    low = jnp.where(lane < 2 * heads, value - high, 0.0)
    return jnp.where(lane < heads, high, low).astype(BF16)


def silu_of_half(half):
    return half + half * jnp.tanh(half)


def spread_matrix(ref, first_head, heads):
    width = ref.shape[1]
    rows = lax.broadcasted_iota(jnp.int32, (LANES, width), 0) & (heads - 1)
    cols = lax.broadcasted_iota(jnp.int32, (LANES, width), 1) >> 6
    ref[...] = jnp.where(rows == cols + first_head, 1.0, 0.0).astype(BF16)


def conv_tile(buf, index, weights, row, rows, code):
    acc = None
    for step in range(KCONV):
        term = buf[index, pl.ds(8 - step + row, rows), :] * weights[REACH - step : KCONV - step]
        if code is not None and step > 0:
            term = jnp.where(code >= step, term, 0.0)
        acc = term if acc is None else acc + term
    return acc


def tail_kernel(seg_s, x_ref, b_ref, c_ref, out_ref):
    rows = seg_s.shape[0]
    start = 0
    for ref in (x_ref, b_ref, c_ref):
        width = ref.shape[1]
        value = ref[...].astype(F32)
        out_ref[:, start : start + width] = value[16 - REACH :].astype(BF16)
        start += width
    ids = [jnp.full((1, LANES), seg_s[rows - REACH + k] + 1, jnp.int32).astype(F32) for k in range(REACH)]
    out_ref[:, start:] = jnp.concatenate(ids, axis=0).astype(BF16)


def decay_kernel(dt_ref, bias_ref, a_log_ref, skip_ref, a_ref, e_ref, w_ref, em_ref):
    heads = dt_ref.shape[1]
    copies = LANES // heads
    wide = lambda value: jnp.concatenate([value] * copies, axis=1)
    z = wide(dt_ref[...].astype(F32)) + wide(bias_ref[...])
    dt = jnp.maximum(z, 0.0) + jnp.log1p(jnp.exp(-jnp.abs(z)))
    fall = -dt * wide(jnp.exp(a_log_ref[...]))
    rows = lax.broadcasted_iota(jnp.int32, (L, L), 0)
    cols = lax.broadcasted_iota(jnp.int32, (L, L), 1)
    lower = jnp.where(rows >= cols, 1.0, 0.0)
    sums = lambda value: jnp.dot(lower, value, precision=lax.Precision.HIGHEST, preferred_element_type=F32)
    upper_half = sums(fall[:L])
    cum = jnp.concatenate([upper_half, sums(fall[L:]) + upper_half[L - 1 : L]], axis=0)
    middle = 0.5 * cum[SPAN - 1 : SPAN]
    a_ref[...] = split_high_low(jnp.exp(middle - cum) * dt, heads)
    e_ref[...] = split_high_low(jnp.exp(cum - middle), heads)
    w_ref[...] = split_high_low(wide(skip_ref[...]) / dt, heads)
    em_ref[0] = split_high_low(jnp.broadcast_to(jnp.exp(middle), (16, LANES)), heads)


def score_kernel(
    seg_s, b_ref, c_ref, halo_ref, ids_ref, wb_ref, wc_ref, seg_ref,
    m_ref, bt_ref, code_ref, info_ref,
    bc_buf, seg_buf, held, *, parts
):
    span = pl.program_id(0)
    width = parts * N
    pieces = width // LANES
    ids = ids_ref[...].astype(F32)
    start = span * SPAN
    first = seg_s[start]
    last = seg_s[start + SPAN - 1]
    oldest_device = (jnp.max(ids[0:1]) - 1.0).astype(jnp.int32)
    before_device = (jnp.max(ids[REACH - 1 : REACH]) - 1.0).astype(jnp.int32)
    before = jnp.where(span == 0, before_device, seg_s[jnp.maximum(start - 1, 0)])
    oldest = jnp.where(span == 0, oldest_device, seg_s[jnp.maximum(start - REACH, 0)])
    cut = (first != last) | ((oldest != first) & (oldest >= 0))
    info_ref[2 * span] = cut.astype(jnp.int32)
    info_ref[2 * span + 1] = (before == last).astype(jnp.int32)

    @pl.when(span == 0)
    def _():
        seg_buf[8 - REACH : 8, :] = ids - 1.0
        for piece in range(2 * pieces):
            bc_buf[piece, 8 - REACH : 8, :] = halo_ref[:, piece * LANES : (piece + 1) * LANES].astype(F32)

    @pl.when(span > 0)
    def _():
        seg_buf[0:8, :] = seg_buf[SPAN : SPAN + 8, :]
        for piece in range(2 * pieces):
            bc_buf[piece, 0:8, :] = bc_buf[piece, SPAN : SPAN + 8, :]

    seg_rows, seg_cols = [], []
    for half in range(2):
        seg_row = seg_ref[:, half * L : (half + 1) * L].astype(F32)
        seg_col = jnp.transpose(jnp.broadcast_to(seg_row, (L, L)))
        seg_rows.append(seg_row)
        seg_cols.append(seg_col)
        seg_buf[8 + half * L : 8 + (half + 1) * L, :] = seg_col[:, :LANES]
    for half in range(2):
        code = jnp.zeros((L, LANES), F32)
        for step in range(1, KCONV):
            same = seg_buf[pl.ds(8 - step + half * L, L), :] == seg_cols[half][:, :LANES]
            code = code + jnp.where(same, 1.0, 0.0)
        code_ref[half * L : (half + 1) * L, :] = code

    weights_b = 0.5 * wb_ref[...].astype(F32)
    weights_c = 0.5 * wc_ref[...].astype(F32)
    for piece in range(pieces):
        lanes = slice(piece * LANES, (piece + 1) * LANES)
        bc_buf[piece, 8 : 8 + SPAN, :] = b_ref[:, lanes].astype(F32)
        bc_buf[pieces + piece, 8 : 8 + SPAN, :] = c_ref[:, lanes].astype(F32)
        for index, weights in ((piece, weights_b), (pieces + piece, weights_c)):
            for row in range(0, SPAN, TILE):
                acc = conv_tile(bc_buf, index, weights[:, lanes], row, TILE, code_ref[row : row + TILE, :])
                held[index, row : row + TILE, :] = silu_of_half(acc)

    rows = lax.broadcasted_iota(jnp.int32, (L, L), 0)
    cols = lax.broadcasted_iota(jnp.int32, (L, L), 1)
    causal = rows >= cols
    across = (((1,), (1,)), ((), ()))
    for g in range(parts):
        per = N // LANES

        def take(first_piece, half):
            parts_ = [held[first_piece + k, half * L : (half + 1) * L, :] for k in range(per)]
            return jnp.concatenate(parts_, axis=1)

        bs = [take(g * per, half) for half in range(2)]
        cs = [take(pieces + g * per, half) for half in range(2)]
        bs16 = [value.astype(BF16) for value in bs]
        cs16 = [value.astype(BF16) for value in cs]
        for half in range(2):
            own = slice(half * L, (half + 1) * L)
            scores = lax.dot_general(cs16[half], bs16[half], across, preferred_element_type=F32)
            allowed = causal & (seg_cols[half] == seg_rows[half])
            m_ref[g, own, 0:L] = jnp.where(allowed, scores, 0.0).astype(BF16)
            enters = seg_cols[half] == before.astype(F32)
            m_ref[g, own, L : L + N] = jnp.where(enters, cs[half], 0.0).astype(BF16)
            latest = seg_cols[half] == last.astype(F32)
            bt_ref[g, :, own] = jnp.transpose(jnp.where(latest, bs[half], 0.0)).astype(BF16)
        scores = lax.dot_general(cs16[1], bs16[0], across, preferred_element_type=F32)
        m_ref[g, L:SPAN, L + N :] = jnp.where(seg_cols[1] == seg_rows[0], scores, 0.0).astype(BF16)
        m_ref[g, 0:L, L + N :] = jnp.zeros((L, L), BF16)


def state_kernel(
    info_ref, x_ref, halo_ref, w_ref, bt_ref, a_ref, em_ref, code_ref,
    u_ref, state_ref, first_ref, factor_ref,
    buf, carry, spread, *, first_head, heads
):
    span = pl.program_id(1)
    width = x_ref.shape[1]
    chunks = width // CHUNK
    inner = CHUNK // LANES
    cut = info_ref[2 * span] > 0

    @pl.when(span == 0)
    def _():
        spread_matrix(spread, first_head + pl.program_id(0) * (width // P_SIZE), heads)
        for piece in range(width // LANES):
            buf[piece, 8 - REACH : 8, :] = halo_ref[:, piece * LANES : (piece + 1) * LANES].astype(F32)

    @pl.when(span > 0)
    def _():
        buf[:, 0:8, :] = buf[:, SPAN : SPAN + 8, :]

    def convolve(masked):
        for chunk in range(chunks):
            cols = slice(chunk * CHUNK, (chunk + 1) * CHUNK)
            scale = dot(a_ref[...], spread[:, cols])
            for piece in range(inner):
                index = chunk * inner + piece
                lanes = slice(index * LANES, (index + 1) * LANES)
                weights = 0.5 * w_ref[:, lanes].astype(F32)
                buf[index, 8 : 8 + SPAN, :] = x_ref[:, lanes].astype(F32)
                for row in range(0, SPAN, TILE):
                    code = code_ref[row : row + TILE, :] if masked else None
                    acc = conv_tile(buf, index, weights, row, TILE, code)
                    factor = scale[row : row + TILE, piece * LANES : (piece + 1) * LANES]
                    u_ref[row : row + TILE, lanes] = (silu_of_half(acc) * factor).astype(BF16)
            grown = dot(bt_ref[0], u_ref[:, cols])
            carry[span, :, cols] = grown

    @pl.when(cut)
    def _():
        convolve(True)

    @pl.when(jnp.logical_not(cut))
    def _():
        convolve(False)

    @pl.when(span == 1)
    def _():
        passes = [info_ref[2 * k + 1].astype(F32) for k in range(2)]
        for chunk in range(chunks):
            cols = slice(chunk * CHUNK, (chunk + 1) * CHUNK)
            early, late = (dot(em_ref[k], spread[:, cols])[0:1] for k in range(2))
            middle = early * carry[0, :, cols]
            first_ref[:, cols] = middle.astype(BF16)
            state_ref[:, cols] = (late * carry[1, :, cols] + (passes[1] * late * late) * middle).astype(BF16)
            factor_ref[:, cols] = (passes[0] * passes[1]) * (early * early * late * late)


def final_kernel(
    info_ref, u_ref, u_first_ref, gate_ref, m_ref, e_ref, w_ref, em_ref, first_ref, t0_ref, t1_ref, t2_ref, gain_ref,
    out_ref,
    enter, spread, held, *, first_head, heads
):
    block = pl.program_id(0)
    width = u_ref.shape[1]
    chunks = width // CHUNK
    spans = [slice(chunk * CHUNK, (chunk + 1) * CHUNK) for chunk in range(chunks)]

    @pl.when(block == 0)
    def _():
        spread_matrix(spread, first_head, heads)
        passes = info_ref[1].astype(F32)
        for cols in spans:
            early, late = (dot(em_ref[k], spread[:, cols])[0:1] for k in range(2))
            came = t0_ref[:, cols].astype(F32) + t1_ref[:, cols].astype(F32) + t2_ref[:, cols].astype(F32)
            enter[0, :, cols] = (early * came).astype(BF16)
            grown = first_ref[:, cols].astype(F32) + (passes * early * early) * came
            enter[1, :, cols] = (late * grown).astype(BF16)

    def rows(odd):
        squares = jnp.zeros((L, LANES), F32)
        for cols in spans:
            part = spread[:, cols]
            u = u_ref[:, cols]
            total = dot(m_ref[0, :, 0:L], u) + dot(m_ref[0, :, L : L + N], enter[block // 2, :, cols])
            if odd:
                total = total + dot(m_ref[0, :, L + N :], u_first_ref[:, cols])
            y = dot(e_ref[...], part) * (total + dot(w_ref[...], part) * u.astype(F32))
            v = y * silu_of_half(0.5 * gate_ref[:, cols].astype(F32))
            held[:, cols] = v
            v2 = v * v
            for piece in range(CHUNK // LANES):
                squares = squares + v2[:, piece * LANES : (piece + 1) * LANES]
        mean = jnp.sum(squares, axis=1, keepdims=True) * (1.0 / width)
        scale = lax.rsqrt(mean + 1e-05)
        for cols in spans:
            out_ref[:, cols] = (held[:, cols] * scale * gain_ref[:, cols]).astype(BF16)

    @pl.when(block % 2 == 0)
    def _():
        rows(False)

    @pl.when(block % 2 == 1)
    def _():
        rows(True)


def final_into_kernel(*refs, first_head, heads):
    final_kernel(*refs[:13], *refs[14:], first_head=first_head, heads=heads)


def per_device(
    x_in, gate_in, b_in, c_in, dt_raw, conv_x, conv_b, conv_c, dt_bias, a_log, skip, norm_gain, segment
):
    rows, channels = x_in.shape
    width_bc = b_in.shape[1]
    parts = width_bc // N
    width = channels // parts
    heads = width // P_SIZE
    all_heads = dt_raw.shape[1]
    blocks = rows // L
    spans = rows // SPAN
    assert spans == 2
    devices = lax.axis_size("req")
    step_width = width // 2
    shape = jax.ShapeDtypeStruct
    smem = pl.BlockSpec(memory_space=pltpu.SMEM)
    whole = lambda *_: (0, 0)
    at_row = lambda k, *_: (k, 0)

    def params(axes):
        return pltpu.CompilerParams(dimension_semantics=("arbitrary",) * axes, vmem_limit_bytes=30 << 20)

    def cost(flops, mib):
        return pl.CostEstimate(flops=flops, bytes_accessed=mib << 20, transcendentals=0)

    shift = [(k, k + 1) for k in range(devices - 1)]
    inside = [(k, k + 1) for k in range(0, devices - 1, 2)]
    across = [(k, k + 1) for k in range(1, devices - 1, 2)]

    last_rows = lambda *_: (rows // 16 - 1, 0)
    tail_width = channels + 2 * width_bc + LANES
    tail = pl.pallas_call(
        tail_kernel,
        grid=(1,),
        in_specs=[
            smem,
            pl.BlockSpec((16, channels), last_rows),
            pl.BlockSpec((16, width_bc), last_rows),
            pl.BlockSpec((16, width_bc), last_rows),
        ],
        out_specs=pl.BlockSpec((REACH, tail_width), whole),
        out_shape=shape((REACH, tail_width), BF16),
        compiler_params=params(1),
        cost_estimate=cost(1000, 0),
        name="tails",
    )(segment, x_in, b_in, c_in)
    halo = lax.ppermute(tail, "req", shift)

    row = lambda value: value.reshape(1, -1)
    narrow = pl.BlockSpec((SPAN, LANES), at_row)
    a_hl, e_hl, w_hl, em = pl.pallas_call(
        decay_kernel,
        grid=(spans,),
        in_specs=[pl.BlockSpec((SPAN, all_heads), at_row)] + [pl.BlockSpec((1, all_heads), whole)] * 3,
        out_specs=[narrow, narrow, narrow, pl.BlockSpec((1, 16, LANES), lambda k: (k, 0, 0))],
        out_shape=[shape((rows, LANES), BF16)] * 3 + [shape((spans, 16, LANES), BF16)],
        compiler_params=params(1),
        cost_estimate=cost(3 * 10**9, 1),
        name="decays",
    )(dt_raw, row(dt_bias), row(a_log), row(skip))

    m, bt, code, info = pl.pallas_call(
        functools.partial(score_kernel, parts=parts),
        grid=(spans,),
        in_specs=[
            smem,
            pl.BlockSpec((SPAN, width_bc), at_row),
            pl.BlockSpec((SPAN, width_bc), at_row),
            pl.BlockSpec((REACH, 2 * width_bc), lambda *_: (0, channels // (2 * width_bc))),
            pl.BlockSpec((REACH, LANES), lambda *_: (0, tail_width // LANES - 1)),
            pl.BlockSpec((KCONV, width_bc), whole),
            pl.BlockSpec((KCONV, width_bc), whole),
            pl.BlockSpec((1, SPAN), lambda k: (0, k)),
        ],
        out_specs=[
            pl.BlockSpec((parts, SPAN, N + SPAN), lambda k: (0, k, 0)),
            pl.BlockSpec((parts, N, SPAN), lambda k: (0, 0, k)),
            narrow,
            smem,
        ],
        out_shape=[
            shape((parts, rows, N + SPAN), BF16),
            shape((parts, N, rows), BF16),
            shape((rows, LANES), F32),
            shape((2 * spans,), jnp.int32),
        ],
        scratch_shapes=[
            pltpu.VMEM((2 * width_bc // LANES, SPAN + 8, LANES), F32),
            pltpu.VMEM((SPAN + 8, LANES), F32),
            pltpu.VMEM((2 * width_bc // LANES, SPAN, LANES), F32),
        ],
        compiler_params=params(1),
        cost_estimate=cost(2 * 10**9, 6),
        name="scores",
    )(segment, b_in, c_in, halo, halo, conv_b, conv_c, row(segment))

    em_spec = lambda: pl.BlockSpec((spans, 16, LANES), lambda *_: (0, 0, 0))

    def local(g):
        steps = width // step_width
        at_cols = lambda j, k: (0, g * steps + j)
        return pl.pallas_call(
            functools.partial(state_kernel, first_head=g * heads, heads=all_heads),
            grid=(steps, spans),
            in_specs=[
                smem,
                pl.BlockSpec((SPAN, step_width), lambda j, k: (k, g * steps + j)),
                pl.BlockSpec((REACH, step_width), at_cols),
                pl.BlockSpec((KCONV, step_width), at_cols),
                pl.BlockSpec((1, N, SPAN), lambda j, k: (g, 0, k)),
                pl.BlockSpec((SPAN, LANES), lambda j, k: (k, 0)),
                em_spec(),
                pl.BlockSpec((SPAN, LANES), lambda j, k: (k, 0)),
            ],
            out_specs=[
                pl.BlockSpec((SPAN, step_width), lambda j, k: (k, j)),
                pl.BlockSpec((N, step_width), lambda j, k: (0, j)),
                pl.BlockSpec((N, step_width), lambda j, k: (0, j)),
                pl.BlockSpec((1, step_width), lambda j, k: (0, j)),
            ],
            out_shape=[
                shape((rows, width), BF16),
                shape((N, width), BF16),
                shape((N, width), BF16),
                shape((1, width), F32),
            ],
            scratch_shapes=[
                pltpu.VMEM((step_width // LANES, SPAN + 8, LANES), F32),
                pltpu.VMEM((spans, N, step_width), F32),
                pltpu.VMEM((LANES, step_width), BF16),
            ],
            compiler_params=params(2),
            cost_estimate=cost(6 * 10**9, 10),
            name="state",
        )(info, x_in, halo, conv_x, bt, a_hl, em, code)

    def travel(state, factor):
        def scaled(value):
            return factor * value.astype(F32)

        first = lax.ppermute(state, "req", inside)
        leaving = (state.astype(F32) + scaled(first)).astype(BF16)
        entering, passed = jnp.zeros_like(state), jnp.zeros_like(state)
        rounds = devices // 2 - 1
        for turn in range(rounds):
            entering = lax.ppermute(leaving, "req", across)
            passed = lax.ppermute(scaled(entering).astype(BF16), "req", inside)
            if turn < rounds - 1:
                leaving = (state.astype(F32) + scaled(first.astype(F32) + passed.astype(F32))).astype(BF16)
        return first, entering, passed

    def final(g, u, first, carries, out):
        at_group = lambda *_: (0, g)
        own = pl.BlockSpec((L, width), lambda k: (k, g))
        square = pl.BlockSpec((N, width), whole)
        in_specs = [
            smem,
            pl.BlockSpec((L, width), at_row),
            pl.BlockSpec((L, width), lambda k: (k // 2 * 2, 0)),
            own,
            pl.BlockSpec((1, L, N + SPAN), lambda k: (g, k, 0)),
            pl.BlockSpec((L, LANES), at_row),
            pl.BlockSpec((L, LANES), at_row),
            em_spec(),
            square,
            square,
            square,
            square,
            pl.BlockSpec((1, width), at_group),
        ]
        operands = [info, u, u, gate_in, m, e_hl, w_hl, em, first, *carries, row(norm_gain)]
        if out is not None:
            in_specs.append(pl.BlockSpec(memory_space=pl.ANY))
            operands.append(out)
        return pl.pallas_call(
            functools.partial(final_kernel if out is None else final_into_kernel, first_head=g * heads, heads=all_heads),
            grid=(blocks,),
            in_specs=in_specs,
            out_specs=own,
            out_shape=shape((rows, channels), BF16),
            scratch_shapes=[
                pltpu.VMEM((spans, N, width), BF16),
                pltpu.VMEM((LANES, width), BF16),
                pltpu.VMEM((L, width), F32),
            ],
            input_output_aliases={} if out is None else {13: 0},
            compiler_params=params(1),
            cost_estimate=cost(6 * 10**9, 16),
            name="final",
        )(*operands)

    locals_ = [local(g) for g in range(parts)]
    carries = [travel(state, factor) for _, state, _, factor in locals_]
    out = None
    for g in range(parts):
        out = final(g, locals_[g][0], locals_[g][2], carries[g], out)
    return out


def solution(mesh):
    rows = P(("groups", "req"), "tp")
    placed = (rows,) * 5 + (P(None, "tp"),) * 3 + (P("tp"),) * 4 + (P(("groups", "req")),)
    return jax.shard_map(
        per_device,
        mesh=mesh,
        in_specs=placed,
        out_specs=rows,
        check_vma=False,
    )
```

```python
import functools

import jax
import jax.numpy as jnp
from jax import lax
from jax.experimental import pallas as pl
from jax.experimental.pallas import tpu as pltpu
from jax.sharding import PartitionSpec as P

P_SIZE = 64
N = 256
L = 256
SPAN = 2 * L
KCONV = 4
REACH = KCONV - 1
LANES = 128
CHUNK = 256
TILE = 128
F32 = jnp.float32
BF16 = jnp.bfloat16


def dot(a, b):
    return jnp.dot(a, b, preferred_element_type=F32)


def split_high_low(value, heads):
    lane = lax.broadcasted_iota(jnp.int32, value.shape, 1)
    high = value.astype(BF16).astype(F32)
    low = jnp.where(lane < 2 * heads, value - high, 0.0)
    return jnp.where(lane < heads, high, low).astype(BF16)


def silu_of_half(half):
    return half + half * jnp.tanh(half)


def spread_matrix(ref, first_head, heads):
    width = ref.shape[1]
    rows = lax.broadcasted_iota(jnp.int32, (LANES, width), 0) & (heads - 1)
    cols = lax.broadcasted_iota(jnp.int32, (LANES, width), 1) >> 6
    ref[...] = jnp.where(rows == cols + first_head, 1.0, 0.0).astype(BF16)


def conv_tile(buf, index, weights, row, rows, code):
    acc = None
    for step in range(KCONV):
        term = buf[index, pl.ds(8 - step + row, rows), :] * weights[REACH - step : KCONV - step]
        if code is not None and step > 0:
            term = jnp.where(code >= step, term, 0.0)
        acc = term if acc is None else acc + term
    return acc


def tail_kernel(seg_s, x_ref, b_ref, c_ref, out_ref):
    rows = seg_s.shape[0]
    start = 0
    for ref in (x_ref, b_ref, c_ref):
        width = ref.shape[1]
        value = ref[...].astype(F32)
        out_ref[:, start : start + width] = value[16 - REACH :].astype(BF16)
        start += width
    ids = [jnp.full((1, LANES), seg_s[rows - REACH + k] + 1, jnp.int32).astype(F32) for k in range(REACH)]
    out_ref[:, start:] = jnp.concatenate(ids, axis=0).astype(BF16)


def decay_kernel(dt_ref, bias_ref, a_log_ref, skip_ref, a_ref, e_ref, w_ref, em_ref):
    heads = dt_ref.shape[1]
    copies = LANES // heads
    wide = lambda value: jnp.concatenate([value] * copies, axis=1)
    z = wide(dt_ref[...].astype(F32)) + wide(bias_ref[...])
    dt = jnp.maximum(z, 0.0) + jnp.log1p(jnp.exp(-jnp.abs(z)))
    fall = -dt * wide(jnp.exp(a_log_ref[...]))
    rows = lax.broadcasted_iota(jnp.int32, (L, L), 0)
    cols = lax.broadcasted_iota(jnp.int32, (L, L), 1)
    lower = jnp.where(rows >= cols, 1.0, 0.0)
    sums = lambda value: jnp.dot(lower, value, precision=lax.Precision.HIGHEST, preferred_element_type=F32)
    upper_half = sums(fall[:L])
    cum = jnp.concatenate([upper_half, sums(fall[L:]) + upper_half[L - 1 : L]], axis=0)
    middle = 0.5 * cum[SPAN - 1 : SPAN]
    a_ref[...] = split_high_low(jnp.exp(middle - cum) * dt, heads)
    e_ref[...] = split_high_low(jnp.exp(cum - middle), heads)
    w_ref[...] = split_high_low(wide(skip_ref[...]) / dt, heads)
    em_ref[0] = split_high_low(jnp.broadcast_to(jnp.exp(middle), (16, LANES)), heads)


def score_kernel(
    seg_s, b_ref, c_ref, halo_ref, ids_ref, wb_ref, wc_ref, seg_ref,
    m_ref, bt_ref, code_ref, info_ref,
    bc_buf, seg_buf, held, *, parts
):
    span = pl.program_id(0)
    width = parts * N
    pieces = width // LANES
    ids = ids_ref[...].astype(F32)
    start = span * SPAN
    first = seg_s[start]
    last = seg_s[start + SPAN - 1]
    oldest_device = (jnp.max(ids[0:1]) - 1.0).astype(jnp.int32)
    before_device = (jnp.max(ids[REACH - 1 : REACH]) - 1.0).astype(jnp.int32)
    before = jnp.where(span == 0, before_device, seg_s[jnp.maximum(start - 1, 0)])
    oldest = jnp.where(span == 0, oldest_device, seg_s[jnp.maximum(start - REACH, 0)])
    cut = (first != last) | ((oldest != first) & (oldest >= 0))
    info_ref[2 * span] = cut.astype(jnp.int32)
    info_ref[2 * span + 1] = (before == last).astype(jnp.int32)

    @pl.when(span == 0)
    def _():
        seg_buf[8 - REACH : 8, :] = ids - 1.0
        for piece in range(2 * pieces):
            bc_buf[piece, 8 - REACH : 8, :] = halo_ref[:, piece * LANES : (piece + 1) * LANES].astype(F32)

    @pl.when(span > 0)
    def _():
        seg_buf[0:8, :] = seg_buf[SPAN : SPAN + 8, :]
        for piece in range(2 * pieces):
            bc_buf[piece, 0:8, :] = bc_buf[piece, SPAN : SPAN + 8, :]

    seg_rows, seg_cols = [], []
    for half in range(2):
        seg_row = seg_ref[:, half * L : (half + 1) * L].astype(F32)
        seg_col = jnp.transpose(jnp.broadcast_to(seg_row, (L, L)))
        seg_rows.append(seg_row)
        seg_cols.append(seg_col)
        seg_buf[8 + half * L : 8 + (half + 1) * L, :] = seg_col[:, :LANES]
    for half in range(2):
        code = jnp.zeros((L, LANES), F32)
        for step in range(1, KCONV):
            same = seg_buf[pl.ds(8 - step + half * L, L), :] == seg_cols[half][:, :LANES]
            code = code + jnp.where(same, 1.0, 0.0)
        code_ref[half * L : (half + 1) * L, :] = code

    weights_b = 0.5 * wb_ref[...].astype(F32)
    weights_c = 0.5 * wc_ref[...].astype(F32)
    for piece in range(pieces):
        lanes = slice(piece * LANES, (piece + 1) * LANES)
        bc_buf[piece, 8 : 8 + SPAN, :] = b_ref[:, lanes].astype(F32)
        bc_buf[pieces + piece, 8 : 8 + SPAN, :] = c_ref[:, lanes].astype(F32)
        for index, weights in ((piece, weights_b), (pieces + piece, weights_c)):
            for row in range(0, SPAN, TILE):
                acc = conv_tile(bc_buf, index, weights[:, lanes], row, TILE, code_ref[row : row + TILE, :])
                held[index, row : row + TILE, :] = silu_of_half(acc)

    rows = lax.broadcasted_iota(jnp.int32, (L, L), 0)
    cols = lax.broadcasted_iota(jnp.int32, (L, L), 1)
    causal = rows >= cols
    across = (((1,), (1,)), ((), ()))
    for g in range(parts):
        per = N // LANES

        def take(first_piece, half):
            parts_ = [held[first_piece + k, half * L : (half + 1) * L, :] for k in range(per)]
            return jnp.concatenate(parts_, axis=1)

        bs = [take(g * per, half) for half in range(2)]
        cs = [take(pieces + g * per, half) for half in range(2)]
        bs16 = [value.astype(BF16) for value in bs]
        cs16 = [value.astype(BF16) for value in cs]
        for half in range(2):
            own = slice(half * L, (half + 1) * L)
            scores = lax.dot_general(cs16[half], bs16[half], across, preferred_element_type=F32)
            allowed = causal & (seg_cols[half] == seg_rows[half])
            m_ref[g, own, 0:L] = jnp.where(allowed, scores, 0.0).astype(BF16)
            enters = seg_cols[half] == before.astype(F32)
            m_ref[g, own, L : L + N] = jnp.where(enters, cs[half], 0.0).astype(BF16)
            latest = seg_cols[half] == last.astype(F32)
            bt_ref[g, :, own] = jnp.transpose(jnp.where(latest, bs[half], 0.0)).astype(BF16)
        scores = lax.dot_general(cs16[1], bs16[0], across, preferred_element_type=F32)
        m_ref[g, L:SPAN, L + N :] = jnp.where(seg_cols[1] == seg_rows[0], scores, 0.0).astype(BF16)
        m_ref[g, 0:L, L + N :] = jnp.zeros((L, L), BF16)


def state_kernel(
    info_ref, x_ref, halo_ref, w_ref, bt_ref, a_ref, em_ref, code_ref,
    u_ref, state_ref, first_ref, factor_ref,
    buf, carry, spread, *, first_head, heads
):
    span = pl.program_id(1)
    width = x_ref.shape[1]
    chunks = width // CHUNK
    inner = CHUNK // LANES
    cut = info_ref[2 * span] > 0

    @pl.when(span == 0)
    def _():
        spread_matrix(spread, first_head + pl.program_id(0) * (width // P_SIZE), heads)
        for piece in range(width // LANES):
            buf[piece, 8 - REACH : 8, :] = halo_ref[:, piece * LANES : (piece + 1) * LANES].astype(F32)

    @pl.when(span > 0)
    def _():
        buf[:, 0:8, :] = buf[:, SPAN : SPAN + 8, :]

    def convolve(masked):
        for chunk in range(chunks):
            cols = slice(chunk * CHUNK, (chunk + 1) * CHUNK)
            scale = dot(a_ref[...], spread[:, cols])
            for piece in range(inner):
                index = chunk * inner + piece
                lanes = slice(index * LANES, (index + 1) * LANES)
                weights = 0.5 * w_ref[:, lanes].astype(F32)
                buf[index, 8 : 8 + SPAN, :] = x_ref[:, lanes].astype(F32)
                for row in range(0, SPAN, TILE):
                    code = code_ref[row : row + TILE, :] if masked else None
                    acc = conv_tile(buf, index, weights, row, TILE, code)
                    factor = scale[row : row + TILE, piece * LANES : (piece + 1) * LANES]
                    u_ref[row : row + TILE, lanes] = (silu_of_half(acc) * factor).astype(BF16)
            grown = dot(bt_ref[0], u_ref[:, cols])
            carry[span, :, cols] = grown

    @pl.when(cut)
    def _():
        convolve(True)

    @pl.when(jnp.logical_not(cut))
    def _():
        convolve(False)

    @pl.when(span == 1)
    def _():
        passes = [info_ref[2 * k + 1].astype(F32) for k in range(2)]
        for chunk in range(chunks):
            cols = slice(chunk * CHUNK, (chunk + 1) * CHUNK)
            early, late = (dot(em_ref[k], spread[:, cols])[0:1] for k in range(2))
            middle = early * carry[0, :, cols]
            first_ref[:, cols] = middle.astype(BF16)
            state_ref[:, cols] = (late * carry[1, :, cols] + (passes[1] * late * late) * middle).astype(BF16)
            factor_ref[:, cols] = (passes[0] * passes[1]) * (early * early * late * late)


def final_kernel(
    info_ref, u_ref, u_first_ref, gate_ref, m_ref, e_ref, w_ref, em_ref, first_ref, t0_ref, t1_ref, t2_ref, gain_ref,
    out_ref,
    enter, spread, held, *, first_head, heads
):
    block = pl.program_id(0)
    width = u_ref.shape[1]
    chunks = width // CHUNK
    spans = [slice(chunk * CHUNK, (chunk + 1) * CHUNK) for chunk in range(chunks)]

    @pl.when(block == 0)
    def _():
        spread_matrix(spread, first_head, heads)
        passes = info_ref[1].astype(F32)
        for cols in spans:
            early, late = (dot(em_ref[k], spread[:, cols])[0:1] for k in range(2))
            came = t0_ref[:, cols].astype(F32) + t1_ref[:, cols].astype(F32) + t2_ref[:, cols].astype(F32)
            enter[0, :, cols] = (early * came).astype(BF16)
            grown = first_ref[:, cols].astype(F32) + (passes * early * early) * came
            enter[1, :, cols] = (late * grown).astype(BF16)

    def rows(odd):
        squares = jnp.zeros((L, LANES), F32)
        for cols in spans:
            part = spread[:, cols]
            u = u_ref[:, cols]
            total = dot(m_ref[0, :, 0:L], u) + dot(m_ref[0, :, L : L + N], enter[block // 2, :, cols])
            if odd:
                total = total + dot(m_ref[0, :, L + N :], u_first_ref[:, cols])
            y = dot(e_ref[...], part) * (total + dot(w_ref[...], part) * u.astype(F32))
            v = y * silu_of_half(0.5 * gate_ref[:, cols].astype(F32))
            held[:, cols] = v
            v2 = v * v
            for piece in range(CHUNK // LANES):
                squares = squares + v2[:, piece * LANES : (piece + 1) * LANES]
        mean = jnp.sum(squares, axis=1, keepdims=True) * (1.0 / width)
        scale = lax.rsqrt(mean + 1e-05)
        for cols in spans:
            out_ref[:, cols] = (held[:, cols] * scale * gain_ref[:, cols]).astype(BF16)

    @pl.when(block % 2 == 0)
    def _():
        rows(False)

    @pl.when(block % 2 == 1)
    def _():
        rows(True)


def state_after_kernel(*refs, first_head, heads):
    state_kernel(*refs[:8], *refs[9:], first_head=first_head, heads=heads)


def scale_kernel(value_ref, factor_ref, *refs):
    out_ref = refs[-1]
    for row in range(0, N, 64):
        rows = slice(row, row + 64)
        out_ref[rows] = (factor_ref[...] * value_ref[rows].astype(F32)).astype(BF16)


def final_into_kernel(*refs, first_head, heads):
    final_kernel(*refs[:13], *refs[14:], first_head=first_head, heads=heads)


def per_device(
    x_in, gate_in, b_in, c_in, dt_raw, conv_x, conv_b, conv_c, dt_bias, a_log, skip, norm_gain, segment
):
    rows, channels = x_in.shape
    width_bc = b_in.shape[1]
    parts = width_bc // N
    width = channels // parts
    heads = width // P_SIZE
    all_heads = dt_raw.shape[1]
    blocks = rows // L
    spans = rows // SPAN
    assert spans == 2
    devices = lax.axis_size("req")
    step_width = width // 2
    shape = jax.ShapeDtypeStruct
    smem = pl.BlockSpec(memory_space=pltpu.SMEM)
    whole = lambda *_: (0, 0)
    at_row = lambda k, *_: (k, 0)

    def params(axes):
        return pltpu.CompilerParams(dimension_semantics=("arbitrary",) * axes, vmem_limit_bytes=30 << 20)

    def cost(flops, mib):
        return pl.CostEstimate(flops=flops, bytes_accessed=mib << 20, transcendentals=0)

    x_in, b_in, c_in = (pltpu.with_memory_space_constraint(value, pltpu.HBM) for value in (x_in, b_in, c_in))
    shift = [(k, k + 1) for k in range(devices - 1)]
    inside = [(k, k + 1) for k in range(0, devices - 1, 2)]
    across = [(k, k + 1) for k in range(1, devices - 1, 2)]

    last_rows = lambda *_: (rows // 16 - 1, 0)
    tail_width = channels + 2 * width_bc + LANES
    tail = pl.pallas_call(
        tail_kernel,
        grid=(1,),
        in_specs=[
            smem,
            pl.BlockSpec((16, channels), last_rows),
            pl.BlockSpec((16, width_bc), last_rows),
            pl.BlockSpec((16, width_bc), last_rows),
        ],
        out_specs=pl.BlockSpec((REACH, tail_width), whole),
        out_shape=shape((REACH, tail_width), BF16),
        compiler_params=params(1),
        cost_estimate=cost(1000, 0),
        name="tails",
    )(segment, x_in, b_in, c_in)
    halo = lax.ppermute(tail, "req", shift)

    row = lambda value: value.reshape(1, -1)
    narrow = pl.BlockSpec((SPAN, LANES), at_row)
    a_hl, e_hl, w_hl, em = pl.pallas_call(
        decay_kernel,
        grid=(spans,),
        in_specs=[pl.BlockSpec((SPAN, all_heads), at_row)] + [pl.BlockSpec((1, all_heads), whole)] * 3,
        out_specs=[narrow, narrow, narrow, pl.BlockSpec((1, 16, LANES), lambda k: (k, 0, 0))],
        out_shape=[shape((rows, LANES), BF16)] * 3 + [shape((spans, 16, LANES), BF16)],
        compiler_params=params(1),
        cost_estimate=cost(3 * 10**9, 1),
        name="decays",
    )(dt_raw, row(dt_bias), row(a_log), row(skip))

    m, bt, code, info = pl.pallas_call(
        functools.partial(score_kernel, parts=parts),
        grid=(spans,),
        in_specs=[
            smem,
            pl.BlockSpec((SPAN, width_bc), at_row),
            pl.BlockSpec((SPAN, width_bc), at_row),
            pl.BlockSpec((REACH, 2 * width_bc), lambda *_: (0, channels // (2 * width_bc))),
            pl.BlockSpec((REACH, LANES), lambda *_: (0, tail_width // LANES - 1)),
            pl.BlockSpec((KCONV, width_bc), whole),
            pl.BlockSpec((KCONV, width_bc), whole),
            pl.BlockSpec((1, SPAN), lambda k: (0, k)),
        ],
        out_specs=[
            pl.BlockSpec((parts, SPAN, N + SPAN), lambda k: (0, k, 0)),
            pl.BlockSpec((parts, N, SPAN), lambda k: (0, 0, k)),
            narrow,
            smem,
        ],
        out_shape=[
            shape((parts, rows, N + SPAN), BF16),
            shape((parts, N, rows), BF16),
            shape((rows, LANES), F32),
            shape((2 * spans,), jnp.int32),
        ],
        scratch_shapes=[
            pltpu.VMEM((2 * width_bc // LANES, SPAN + 8, LANES), F32),
            pltpu.VMEM((SPAN + 8, LANES), F32),
            pltpu.VMEM((2 * width_bc // LANES, SPAN, LANES), F32),
        ],
        compiler_params=params(1),
        cost_estimate=cost(2 * 10**9, 6),
        name="scores",
    )(segment, b_in, c_in, halo, halo, conv_b, conv_c, row(segment))

    em_spec = lambda: pl.BlockSpec((spans, 16, LANES), lambda *_: (0, 0, 0))

    anywhere = pl.BlockSpec(memory_space=pl.ANY)

    def local(g, token):
        steps = width // step_width
        at_cols = lambda j, k: (0, g * steps + j)
        return pl.pallas_call(
            functools.partial(state_kernel if token is None else state_after_kernel, first_head=g * heads, heads=all_heads),
            grid=(steps, spans),
            in_specs=[
                smem,
                pl.BlockSpec((SPAN, step_width), lambda j, k: (k, g * steps + j)),
                pl.BlockSpec((REACH, step_width), at_cols),
                pl.BlockSpec((KCONV, step_width), at_cols),
                pl.BlockSpec((1, N, SPAN), lambda j, k: (g, 0, k)),
                pl.BlockSpec((SPAN, LANES), lambda j, k: (k, 0)),
                em_spec(),
                pl.BlockSpec((SPAN, LANES), lambda j, k: (k, 0)),
            ]
            + ([] if token is None else [anywhere]),
            out_specs=[
                pl.BlockSpec((SPAN, step_width), lambda j, k: (k, j)),
                pl.BlockSpec((N, step_width), lambda j, k: (0, j)),
                pl.BlockSpec((N, step_width), lambda j, k: (0, j)),
                pl.BlockSpec((1, step_width), lambda j, k: (0, j)),
            ],
            out_shape=[
                shape((rows, width), BF16),
                shape((N, width), BF16),
                shape((N, width), BF16),
                shape((1, width), F32),
            ],
            scratch_shapes=[
                pltpu.VMEM((step_width // LANES, SPAN + 8, LANES), F32),
                pltpu.VMEM((spans, N, step_width), F32),
                pltpu.VMEM((LANES, step_width), BF16),
            ],
            compiler_params=params(2),
            cost_estimate=cost(6 * 10**9, 10),
            name="state",
        )(info, x_in, halo, conv_x, bt, a_hl, em, code, *([] if token is None else [token]))

    def scaled(value, factor, token):
        tokens = [] if token is None else [token]
        whole_spec = lambda array: pl.BlockSpec(array.shape, whole)
        return pl.pallas_call(
            scale_kernel,
            grid=(1,),
            in_specs=[whole_spec(value), whole_spec(factor)] + [anywhere] * len(tokens),
            out_specs=whole_spec(value),
            out_shape=shape(value.shape, BF16),
            compiler_params=params(1),
            cost_estimate=cost(10**6, 2),
            name="scale",
        )(value, factor, *tokens)

    def leave(state, first, factor):
        return (state.astype(F32) + factor * first.astype(F32)).astype(BF16)

    def travel(state, first, leaving, factor, token):
        entering, passed = jnp.zeros_like(state), jnp.zeros_like(state)
        rounds = devices // 2 - 1
        for turn in range(rounds):
            entering = lax.ppermute(leaving, "req", across)
            passed = lax.ppermute(scaled(entering, factor, token), "req", inside)
            if turn < rounds - 1:
                leaving = leave(state, first.astype(F32) + passed.astype(F32), factor)
        return first, entering, passed

    def final(g, u, first, carries, out):
        at_group = lambda *_: (0, g)
        own = pl.BlockSpec((L, width), lambda k: (k, g))
        square = pl.BlockSpec((N, width), whole)
        in_specs = [
            smem,
            pl.BlockSpec((L, width), at_row),
            pl.BlockSpec((L, width), lambda k: (k // 2 * 2, 0)),
            own,
            pl.BlockSpec((1, L, N + SPAN), lambda k: (g, k, 0)),
            pl.BlockSpec((L, LANES), at_row),
            pl.BlockSpec((L, LANES), at_row),
            em_spec(),
            square,
            square,
            square,
            square,
            pl.BlockSpec((1, width), at_group),
        ]
        operands = [info, u, u, gate_in, m, e_hl, w_hl, em, first, *carries, row(norm_gain)]
        if out is not None:
            in_specs.append(pl.BlockSpec(memory_space=pl.ANY))
            operands.append(out)
        return pl.pallas_call(
            functools.partial(final_kernel if out is None else final_into_kernel, first_head=g * heads, heads=all_heads),
            grid=(blocks,),
            in_specs=in_specs,
            out_specs=own,
            out_shape=shape((rows, channels), BF16),
            scratch_shapes=[
                pltpu.VMEM((spans, N, width), BF16),
                pltpu.VMEM((LANES, width), BF16),
                pltpu.VMEM((L, width), F32),
            ],
            input_output_aliases={} if out is None else {13: 0},
            compiler_params=params(1),
            cost_estimate=cost(6 * 10**9, 16),
            name="final",
        )(*operands)

    leaving, locals_ = None, []
    for g in range(parts):
        u, state, inner, factor = local(g, leaving)
        first = lax.ppermute(state, "req", inside)
        leaving = leave(state, first, factor)
        locals_.append((u, inner, state, first, leaving, factor))
    out = None
    for g in range(parts):
        u, inner, *sent = locals_[g]
        out = final(g, u, inner, travel(*sent, out), out)
    return out


def solution(mesh):
    rows = P(("groups", "req"), "tp")
    placed = (rows,) * 5 + (P(None, "tp"),) * 3 + (P("tp"),) * 4 + (P(("groups", "req")),)
    return jax.shard_map(
        per_device,
        mesh=mesh,
        in_specs=placed,
        out_specs=rows,
        check_vma=False,
    )
```

```python
import functools

import jax
import jax.numpy as jnp
from jax import lax
from jax.experimental import pallas as pl
from jax.experimental.pallas import tpu as pltpu
from jax.sharding import PartitionSpec as P

P_SIZE = 64
N = 256
L = 256
SPAN = 2 * L
KCONV = 4
REACH = KCONV - 1
LANES = 128
CHUNK = 256
TILE = 128
F32 = jnp.float32
BF16 = jnp.bfloat16


def dot(a, b):
    return jnp.dot(a, b, preferred_element_type=F32)


def split_high_low(value, heads):
    lane = lax.broadcasted_iota(jnp.int32, value.shape, 1)
    high = value.astype(BF16).astype(F32)
    low = jnp.where(lane < 2 * heads, value - high, 0.0)
    return jnp.where(lane < heads, high, low).astype(BF16)


def silu_of_half(half):
    return half + half * jnp.tanh(half)


def spread_matrix(ref, first_head, heads):
    width = ref.shape[1]
    rows = lax.broadcasted_iota(jnp.int32, (LANES, width), 0) & (heads - 1)
    cols = lax.broadcasted_iota(jnp.int32, (LANES, width), 1) >> 6
    ref[...] = jnp.where(rows == cols + first_head, 1.0, 0.0).astype(BF16)


def conv_tile(buf, index, weights, row, rows, code):
    acc = None
    for step in range(KCONV):
        term = buf[index, pl.ds(8 - step + row, rows), :] * weights[REACH - step : KCONV - step]
        if code is not None and step > 0:
            term = jnp.where(code >= step, term, 0.0)
        acc = term if acc is None else acc + term
    return acc


def tail_kernel(seg_s, x_ref, b_ref, c_ref, out_ref):
    rows = seg_s.shape[0]
    start = 0
    for ref in (x_ref, b_ref, c_ref):
        width = ref.shape[1]
        value = ref[...].astype(F32)
        out_ref[:, start : start + width] = value[16 - REACH :].astype(BF16)
        start += width
    ids = [jnp.full((1, LANES), seg_s[rows - REACH + k] + 1, jnp.int32).astype(F32) for k in range(REACH)]
    out_ref[:, start:] = jnp.concatenate(ids, axis=0).astype(BF16)


def decay_kernel(dt_ref, bias_ref, a_log_ref, skip_ref, a_ref, e_ref, w_ref, em_ref):
    heads = dt_ref.shape[1]
    copies = LANES // heads
    wide = lambda value: jnp.concatenate([value] * copies, axis=1)
    z = wide(dt_ref[...].astype(F32)) + wide(bias_ref[...])
    dt = jnp.maximum(z, 0.0) + jnp.log1p(jnp.exp(-jnp.abs(z)))
    fall = -dt * wide(jnp.exp(a_log_ref[...]))
    rows = lax.broadcasted_iota(jnp.int32, (L, L), 0)
    cols = lax.broadcasted_iota(jnp.int32, (L, L), 1)
    lower = jnp.where(rows >= cols, 1.0, 0.0)
    sums = lambda value: jnp.dot(lower, value, precision=lax.Precision.HIGHEST, preferred_element_type=F32)
    upper_half = sums(fall[:L])
    cum = jnp.concatenate([upper_half, sums(fall[L:]) + upper_half[L - 1 : L]], axis=0)
    middle = 0.5 * cum[SPAN - 1 : SPAN]
    a_ref[...] = split_high_low(jnp.exp(middle - cum) * dt, heads)
    e_ref[...] = split_high_low(jnp.exp(cum - middle), heads)
    w_ref[...] = split_high_low(wide(skip_ref[...]) / dt, heads)
    em_ref[0] = split_high_low(jnp.broadcast_to(jnp.exp(middle), (16, LANES)), heads)


def fill_conv(buf, held, source, halo_ref, weights_ref, codes, span):
    pieces = source.shape[1] // LANES

    @pl.when(span == 0)
    def _():
        for piece in range(pieces):
            buf[piece, 8 - REACH : 8, :] = halo_ref[:, piece * LANES : (piece + 1) * LANES].astype(F32)

    @pl.when(span > 0)
    def _():
        for piece in range(pieces):
            buf[piece, 0:8, :] = buf[piece, SPAN : SPAN + 8, :]

    weights = 0.5 * weights_ref[...].astype(F32)
    for piece in range(pieces):
        lanes = slice(piece * LANES, (piece + 1) * LANES)
        buf[piece, 8 : 8 + SPAN, :] = source[:, lanes].astype(F32)
        for row in range(0, SPAN, TILE):
            acc = conv_tile(buf, piece, weights[:, lanes], row, TILE, codes[row : row + TILE, :])
            held[row : row + TILE, lanes] = silu_of_half(acc)


def entering_id(ids, k):
    return (jnp.max(ids[k : k + 1]) - 1.0).astype(jnp.int32)


def b_kernel(
    seg_s, b_ref, halo_ref, ids_ref, wb_ref, seg_ref,
    bs_ref, bt_ref, code_ref, info_ref,
    buf, seg_buf, held, *, parts
):
    span = pl.program_id(0)
    ids = ids_ref[...].astype(F32)
    start = span * SPAN
    first = seg_s[start]
    last = seg_s[start + SPAN - 1]
    before = jnp.where(span == 0, entering_id(ids, REACH - 1), seg_s[jnp.maximum(start - 1, 0)])
    oldest = jnp.where(span == 0, entering_id(ids, 0), seg_s[jnp.maximum(start - REACH, 0)])
    cut = (first != last) | ((oldest != first) & (oldest >= 0))
    info_ref[2 * span] = cut.astype(jnp.int32)
    info_ref[2 * span + 1] = (before == last).astype(jnp.int32)

    @pl.when(span == 0)
    def _():
        seg_buf[8 - REACH : 8, :] = ids - 1.0

    @pl.when(span > 0)
    def _():
        seg_buf[0:8, :] = seg_buf[SPAN : SPAN + 8, :]

    seg_row = seg_ref[...].astype(F32)
    seg_buf[8 : 8 + SPAN, :] = jnp.transpose(jnp.broadcast_to(seg_row, (LANES, SPAN)))
    own = seg_buf[8 : 8 + SPAN, :]
    code = jnp.zeros((SPAN, LANES), F32)
    for step in range(1, KCONV):
        code = code + jnp.where(seg_buf[8 - step : 8 - step + SPAN, :] == own, 1.0, 0.0)
    code_ref[...] = code
    fill_conv(buf, held, b_ref, halo_ref, wb_ref, code_ref, span)
    bs_ref[...] = held[...].astype(BF16)
    latest = seg_row == last.astype(F32)
    for g in range(parts):
        bt_ref[g] = jnp.where(latest, jnp.transpose(held[:, g * N : (g + 1) * N]), 0.0).astype(BF16)


def score_kernel(
    seg_s, c_ref, halo_ref, ids_ref, wc_ref, seg_ref, bs_ref, code_ref, token_ref,
    m_ref,
    buf, held, *, parts
):
    del token_ref
    span = pl.program_id(0)
    ids = ids_ref[...].astype(F32)
    start = span * SPAN
    before = jnp.where(span == 0, entering_id(ids, REACH - 1), seg_s[jnp.maximum(start - 1, 0)])
    fill_conv(buf, held, c_ref, halo_ref, wc_ref, code_ref, span)
    halves = [slice(half * L, (half + 1) * L) for half in range(2)]
    seg_rows = [seg_ref[:, half].astype(F32) for half in halves]
    seg_cols = [jnp.transpose(jnp.broadcast_to(seg_row, (L, L))) for seg_row in seg_rows]
    rows = lax.broadcasted_iota(jnp.int32, (L, L), 0)
    cols = lax.broadcasted_iota(jnp.int32, (L, L), 1)
    causal = rows >= cols
    across = (((1,), (1,)), ((), ()))
    for g in range(parts):
        lanes = slice(g * N, (g + 1) * N)
        cs = held[:, lanes].astype(BF16)
        early = lax.dot_general(cs, bs_ref[halves[0], lanes], across, preferred_element_type=F32)
        late = lax.dot_general(cs[L:], bs_ref[halves[1], lanes], across, preferred_element_type=F32)
        allowed = [causal & (seg_cols[half] == seg_rows[half]) for half in range(2)]
        m_ref[g, 0:L, 0:L] = jnp.where(allowed[0], early[:L], 0.0).astype(BF16)
        m_ref[g, L:SPAN, 0:L] = jnp.where(seg_cols[1] == seg_rows[0], early[L:], 0.0).astype(BF16)
        m_ref[g, 0:L, L + N :] = jnp.zeros((L, L), BF16)
        m_ref[g, L:SPAN, L + N :] = jnp.where(allowed[1], late, 0.0).astype(BF16)
        for half in range(2):
            enters = seg_cols[half] == before.astype(F32)
            m_ref[g, halves[half], L : L + N] = jnp.where(enters, held[halves[half], lanes], 0.0).astype(BF16)


def state_kernel(
    info_ref, x_ref, halo_ref, w_ref, bt_ref, a_ref, em_ref, code_ref,
    u_ref, state_ref, first_ref, factor_ref,
    buf, carry, spread, *, first_head, heads
):
    span = pl.program_id(1)
    width = x_ref.shape[1]
    chunks = width // CHUNK
    inner = CHUNK // LANES
    cut = info_ref[2 * span] > 0

    @pl.when(span == 0)
    def _():
        spread_matrix(spread, first_head + pl.program_id(0) * (width // P_SIZE), heads)
        for piece in range(width // LANES):
            buf[piece, 8 - REACH : 8, :] = halo_ref[:, piece * LANES : (piece + 1) * LANES].astype(F32)

    @pl.when(span > 0)
    def _():
        buf[:, 0:8, :] = buf[:, SPAN : SPAN + 8, :]

    def convolve(masked):
        for chunk in range(chunks):
            cols = slice(chunk * CHUNK, (chunk + 1) * CHUNK)
            scale = dot(a_ref[...], spread[:, cols])
            for piece in range(inner):
                index = chunk * inner + piece
                lanes = slice(index * LANES, (index + 1) * LANES)
                weights = 0.5 * w_ref[:, lanes].astype(F32)
                buf[index, 8 : 8 + SPAN, :] = x_ref[:, lanes].astype(F32)
                for row in range(0, SPAN, TILE):
                    code = code_ref[row : row + TILE, :] if masked else None
                    acc = conv_tile(buf, index, weights, row, TILE, code)
                    factor = scale[row : row + TILE, piece * LANES : (piece + 1) * LANES]
                    u_ref[row : row + TILE, lanes] = (silu_of_half(acc) * factor).astype(BF16)
            grown = dot(bt_ref[0], u_ref[:, cols])
            carry[span, :, cols] = grown

    @pl.when(cut)
    def _():
        convolve(True)

    @pl.when(jnp.logical_not(cut))
    def _():
        convolve(False)

    @pl.when(span == 1)
    def _():
        passes = [info_ref[2 * k + 1].astype(F32) for k in range(2)]
        for chunk in range(chunks):
            cols = slice(chunk * CHUNK, (chunk + 1) * CHUNK)
            early, late = (dot(em_ref[k], spread[:, cols])[0:1] for k in range(2))
            middle = early * carry[0, :, cols]
            first_ref[:, cols] = middle.astype(BF16)
            state_ref[:, cols] = (late * carry[1, :, cols] + (passes[1] * late * late) * middle).astype(BF16)
            factor_ref[:, cols] = (passes[0] * passes[1]) * (early * early * late * late)


def final_kernel(
    info_ref, u_ref, gate_ref, m_ref, e_ref, w_ref, em_ref, first_ref, t0_ref, t1_ref, t2_ref, gain_ref,
    out_ref, done_ref,
    enter, spread, held, *, first_head, heads
):
    span = pl.program_id(0)
    width = u_ref.shape[1]
    chunks = width // CHUNK
    strips = [slice(chunk * CHUNK, (chunk + 1) * CHUNK) for chunk in range(chunks)]

    @pl.when(span == 0)
    def _():
        done_ref[...] = jnp.zeros_like(done_ref)
        spread_matrix(spread, first_head, heads)
        passes = info_ref[1].astype(F32)
        for cols in strips:
            early, late = (dot(em_ref[k], spread[:, cols])[0:1] for k in range(2))
            came = t0_ref[:, cols].astype(F32) + t1_ref[:, cols].astype(F32) + t2_ref[:, cols].astype(F32)
            enter[0, :, cols] = (early * came).astype(BF16)
            grown = first_ref[:, cols].astype(F32) + (passes * early * early) * came
            enter[1, :, cols] = (late * grown).astype(BF16)

    squares = [jnp.zeros((L, LANES), F32) for _ in range(2)]
    for cols in strips:
        part = spread[:, cols]
        sources = jnp.concatenate([u_ref[0:L, cols], enter[span, :, cols]], axis=0)
        total = dot(m_ref[0, :, 0 : L + N], sources)
        last = dot(m_ref[0, L:SPAN, L + N :], u_ref[L:SPAN, cols])
        outer = dot(e_ref[...], part)
        direct = dot(w_ref[...], part)
        for half in range(2):
            own = slice(half * L, (half + 1) * L)
            sums = total[own] + direct[own] * u_ref[own, cols].astype(F32)
            if half == 1:
                sums = sums + last
            v = (outer[own] * sums) * silu_of_half(0.5 * gate_ref[own, cols].astype(F32))
            held[own, cols] = v
            v2 = v * v
            for piece in range(CHUNK // LANES):
                squares[half] = squares[half] + v2[:, piece * LANES : (piece + 1) * LANES]
    for half in range(2):
        own = slice(half * L, (half + 1) * L)
        mean = jnp.sum(squares[half], axis=1, keepdims=True) * (1.0 / width)
        scale = lax.rsqrt(mean + 1e-05)
        for cols in strips:
            out_ref[own, cols] = (held[own, cols] * scale * gain_ref[:, cols]).astype(BF16)


def state_after_kernel(*refs, first_head, heads):
    state_kernel(*refs[:8], *refs[10:], first_head=first_head, heads=heads)


def scale_kernel(value_ref, factor_ref, *refs):
    out_ref = refs[-1]
    for row in range(0, N, 64):
        rows = slice(row, row + 64)
        out_ref[rows] = (factor_ref[...] * value_ref[rows].astype(F32)).astype(BF16)


def final_into_kernel(*refs, first_head, heads):
    final_kernel(*refs[:12], *refs[13:], first_head=first_head, heads=heads)


def per_device(
    x_in, gate_in, b_in, c_in, dt_raw, conv_x, conv_b, conv_c, dt_bias, a_log, skip, norm_gain, segment
):
    rows, channels = x_in.shape
    width_bc = b_in.shape[1]
    parts = width_bc // N
    width = channels // parts
    heads = width // P_SIZE
    all_heads = dt_raw.shape[1]
    blocks = rows // L
    spans = rows // SPAN
    assert spans == 2
    devices = lax.axis_size("req")
    step_width = width // 2
    shape = jax.ShapeDtypeStruct
    smem = pl.BlockSpec(memory_space=pltpu.SMEM)
    whole = lambda *_: (0, 0)
    at_row = lambda k, *_: (k, 0)

    def params(axes):
        return pltpu.CompilerParams(dimension_semantics=("arbitrary",) * axes, vmem_limit_bytes=30 << 20)

    def cost(flops, mib):
        return pl.CostEstimate(flops=flops, bytes_accessed=mib << 20, transcendentals=0)

    x_in, b_in, c_in = (pltpu.with_memory_space_constraint(value, pltpu.HBM) for value in (x_in, b_in, c_in))
    shift = [(k, k + 1) for k in range(devices - 1)]
    inside = [(k, k + 1) for k in range(0, devices - 1, 2)]
    across = [(k, k + 1) for k in range(1, devices - 1, 2)]

    last_rows = lambda *_: (rows // 16 - 1, 0)
    tail_width = channels + 2 * width_bc + LANES
    tail = pl.pallas_call(
        tail_kernel,
        grid=(1,),
        in_specs=[
            smem,
            pl.BlockSpec((16, channels), last_rows),
            pl.BlockSpec((16, width_bc), last_rows),
            pl.BlockSpec((16, width_bc), last_rows),
        ],
        out_specs=pl.BlockSpec((REACH, tail_width), whole),
        out_shape=shape((REACH, tail_width), BF16),
        compiler_params=params(1),
        cost_estimate=cost(1000, 0),
        name="tails",
    )(segment, x_in, b_in, c_in)
    halo = lax.ppermute(tail, "req", shift)

    row = lambda value: value.reshape(1, -1)
    narrow = pl.BlockSpec((SPAN, LANES), at_row)
    a_hl, e_hl, w_hl, em = pl.pallas_call(
        decay_kernel,
        grid=(spans,),
        in_specs=[pl.BlockSpec((SPAN, all_heads), at_row)] + [pl.BlockSpec((1, all_heads), whole)] * 3,
        out_specs=[narrow, narrow, narrow, pl.BlockSpec((1, 16, LANES), lambda k: (k, 0, 0))],
        out_shape=[shape((rows, LANES), BF16)] * 3 + [shape((spans, 16, LANES), BF16)],
        compiler_params=params(1),
        cost_estimate=cost(3 * 10**9, 1),
        name="decays",
    )(dt_raw, row(dt_bias), row(a_log), row(skip))

    halo_bc = lambda which: pl.BlockSpec((REACH, width_bc), lambda *_: (0, channels // width_bc + which))
    ids_spec = pl.BlockSpec((REACH, LANES), lambda *_: (0, tail_width // LANES - 1))
    seg_spec = pl.BlockSpec((1, SPAN), lambda k: (0, k))
    wide_bc = pl.BlockSpec((SPAN, width_bc), at_row)
    conv_scratch = [pltpu.VMEM((width_bc // LANES, SPAN + 8, LANES), F32)]
    bs, bt, code, info = pl.pallas_call(
        functools.partial(b_kernel, parts=parts),
        grid=(spans,),
        in_specs=[smem, wide_bc, halo_bc(0), ids_spec, pl.BlockSpec((KCONV, width_bc), whole), seg_spec],
        out_specs=[wide_bc, pl.BlockSpec((parts, N, SPAN), lambda k: (0, 0, k)), narrow, smem],
        out_shape=[
            shape((rows, width_bc), BF16),
            shape((parts, N, rows), BF16),
            shape((rows, LANES), F32),
            shape((2 * spans,), jnp.int32),
        ],
        scratch_shapes=conv_scratch + [pltpu.VMEM((SPAN + 8, LANES), F32), pltpu.VMEM((SPAN, width_bc), F32)],
        compiler_params=params(1),
        cost_estimate=cost(10**9, 3),
        name="b_rows",
    )(segment, b_in, halo, halo, conv_b, row(segment))

    def score(token):
        return pl.pallas_call(
            functools.partial(score_kernel, parts=parts),
            grid=(spans,),
            in_specs=[
                smem, wide_bc, halo_bc(1), ids_spec, pl.BlockSpec((KCONV, width_bc), whole), seg_spec, wide_bc, narrow,
                pl.BlockSpec(memory_space=pl.ANY),
            ],
            out_specs=pl.BlockSpec((parts, SPAN, N + SPAN), lambda k: (0, k, 0)),
            out_shape=shape((parts, rows, N + SPAN), BF16),
            scratch_shapes=conv_scratch + [pltpu.VMEM((SPAN, width_bc), F32)],
            compiler_params=params(1),
            cost_estimate=cost(3 * 10**9, 4),
            name="scores",
        )(segment, c_in, halo, halo, conv_c, row(segment), bs, code, token)

    em_spec = lambda: pl.BlockSpec((spans, 16, LANES), lambda *_: (0, 0, 0))

    anywhere = pl.BlockSpec(memory_space=pl.ANY)

    def local(g, tokens):
        steps = width // step_width
        at_cols = lambda j, k: (0, g * steps + j)
        return pl.pallas_call(
            functools.partial(state_after_kernel if tokens else state_kernel, first_head=g * heads, heads=all_heads),
            grid=(steps, spans),
            in_specs=[
                smem,
                pl.BlockSpec((SPAN, step_width), lambda j, k: (k, g * steps + j)),
                pl.BlockSpec((REACH, step_width), at_cols),
                pl.BlockSpec((KCONV, step_width), at_cols),
                pl.BlockSpec((1, N, SPAN), lambda j, k: (g, 0, k)),
                pl.BlockSpec((SPAN, LANES), lambda j, k: (k, 0)),
                em_spec(),
                pl.BlockSpec((SPAN, LANES), lambda j, k: (k, 0)),
            ]
            + [anywhere] * len(tokens),
            out_specs=[
                pl.BlockSpec((SPAN, step_width), lambda j, k: (k, j)),
                pl.BlockSpec((N, step_width), lambda j, k: (0, j)),
                pl.BlockSpec((N, step_width), lambda j, k: (0, j)),
                pl.BlockSpec((1, step_width), lambda j, k: (0, j)),
            ],
            out_shape=[
                shape((rows, width), BF16),
                shape((N, width), BF16),
                shape((N, width), BF16),
                shape((1, width), F32),
            ],
            scratch_shapes=[
                pltpu.VMEM((step_width // LANES, SPAN + 8, LANES), F32),
                pltpu.VMEM((spans, N, step_width), F32),
                pltpu.VMEM((LANES, step_width), BF16),
            ],
            compiler_params=params(2),
            cost_estimate=cost(6 * 10**9, 10),
            name="state",
        )(info, x_in, halo, conv_x, bt, a_hl, em, code, *tokens)

    def scaled(value, factor, token):
        tokens = [] if token is None else [token]
        whole_spec = lambda array: pl.BlockSpec(array.shape, whole)
        return pl.pallas_call(
            scale_kernel,
            grid=(1,),
            in_specs=[whole_spec(value), whole_spec(factor)] + [anywhere] * len(tokens),
            out_specs=whole_spec(value),
            out_shape=shape(value.shape, BF16),
            compiler_params=params(1),
            cost_estimate=cost(10**6, 2),
            name="scale",
        )(value, factor, *tokens)

    def leave(state, first, factor):
        return (state.astype(F32) + factor * first.astype(F32)).astype(BF16)

    def travel(state, first, leaving, factor, token):
        entering, passed = jnp.zeros_like(state), jnp.zeros_like(state)
        rounds = devices // 2 - 1
        for turn in range(rounds):
            entering = lax.ppermute(leaving, "req", across)
            passed = lax.ppermute(scaled(entering, factor, token), "req", inside)
            if turn < rounds - 1:
                leaving = leave(state, first.astype(F32) + passed.astype(F32), factor)
        return first, entering, passed

    def final(g, u, m, first, carries, out):
        at_group = lambda *_: (0, g)
        own = pl.BlockSpec((SPAN, width), lambda k: (k, g))
        square = pl.BlockSpec((N, width), whole)
        in_specs = [
            smem,
            pl.BlockSpec((SPAN, width), at_row),
            own,
            pl.BlockSpec((1, SPAN, N + SPAN), lambda k: (g, k, 0)),
            narrow,
            narrow,
            em_spec(),
            square,
            square,
            square,
            square,
            pl.BlockSpec((1, width), at_group),
        ]
        operands = [info, u, gate_in, m, e_hl, w_hl, em, first, *carries, row(norm_gain)]
        if out is not None:
            in_specs.append(anywhere)
            operands.append(out)
        return pl.pallas_call(
            functools.partial(final_kernel if out is None else final_into_kernel, first_head=g * heads, heads=all_heads),
            grid=(spans,),
            in_specs=in_specs,
            out_specs=[own, pl.BlockSpec((8, LANES), whole)],
            out_shape=[shape((rows, channels), BF16), shape((8, LANES), F32)],
            scratch_shapes=[
                pltpu.VMEM((spans, N, width), BF16),
                pltpu.VMEM((LANES, width), BF16),
                pltpu.VMEM((SPAN, width), F32),
            ],
            input_output_aliases={} if out is None else {12: 0},
            compiler_params=params(1),
            cost_estimate=cost(6 * 10**9, 16),
            name="final",
        )(*operands)

    leaving, locals_, m = None, [], None
    for g in range(parts):
        u, state, inner, factor = local(g, [leaving, m] if g else [])
        first = lax.ppermute(state, "req", inside)
        if m is None:
            m = score(factor)
        leaving = leave(state, first, factor)
        locals_.append((u, inner, state, first, leaving, factor))
    out = done = None
    for g in range(parts):
        u, inner, *sent = locals_[g]
        out, done = final(g, u, m, inner, travel(*sent, done), out)
    return out


def solution(mesh):
    rows = P(("groups", "req"), "tp")
    placed = (rows,) * 5 + (P(None, "tp"),) * 3 + (P("tp"),) * 4 + (P(("groups", "req")),)
    return jax.shard_map(
        per_device,
        mesh=mesh,
        in_specs=placed,
        out_specs=rows,
        check_vma=False,
    )
```

```python
import functools

import jax
import jax.numpy as jnp
from jax import lax
from jax.experimental import pallas as pl
from jax.experimental.pallas import tpu as pltpu
from jax.sharding import PartitionSpec as P

P_SIZE = 64
N = 256
L = 256
SPAN = 2 * L
KCONV = 4
REACH = KCONV - 1
LANES = 128
CHUNK = 256
TILE = 128
F32 = jnp.float32
BF16 = jnp.bfloat16


def dot(a, b):
    return jnp.dot(a, b, preferred_element_type=F32)


def split_high_low(value, heads):
    lane = lax.broadcasted_iota(jnp.int32, value.shape, 1)
    high = value.astype(BF16).astype(F32)
    low = jnp.where(lane < 2 * heads, value - high, 0.0)
    return jnp.where(lane < heads, high, low).astype(BF16)


def silu_of_half(half):
    return half + half * jnp.tanh(half)


def spread_matrix(ref, first_head, heads):
    width = ref.shape[1]
    rows = lax.broadcasted_iota(jnp.int32, (LANES, width), 0) & (heads - 1)
    cols = lax.broadcasted_iota(jnp.int32, (LANES, width), 1) >> 6
    ref[...] = jnp.where(rows == cols + first_head, 1.0, 0.0).astype(BF16)


def conv_tile(buf, index, weights, row, rows, code):
    acc = None
    for step in range(KCONV):
        term = buf[index, pl.ds(8 - step + row, rows), :] * weights[REACH - step : KCONV - step]
        if code is not None and step > 0:
            term = jnp.where(code >= step, term, 0.0)
        acc = term if acc is None else acc + term
    return acc


def tail_kernel(seg_s, x_ref, b_ref, c_ref, out_ref):
    rows = seg_s.shape[0]
    start = 0
    for ref in (x_ref, b_ref, c_ref):
        width = ref.shape[1]
        value = ref[...].astype(F32)
        out_ref[:, start : start + width] = value[16 - REACH :].astype(BF16)
        start += width
    ids = [jnp.full((1, LANES), seg_s[rows - REACH + k] + 1, jnp.int32).astype(F32) for k in range(REACH)]
    out_ref[:, start:] = jnp.concatenate(ids, axis=0).astype(BF16)


def decay_kernel(dt_ref, bias_ref, a_log_ref, skip_ref, a_ref, e_ref, w_ref, em_ref):
    heads = dt_ref.shape[1]
    copies = LANES // heads
    wide = lambda value: jnp.concatenate([value] * copies, axis=1)
    z = wide(dt_ref[...].astype(F32)) + wide(bias_ref[...])
    dt = jnp.maximum(z, 0.0) + jnp.log1p(jnp.exp(-jnp.abs(z)))
    fall = -dt * wide(jnp.exp(a_log_ref[...]))
    rows = lax.broadcasted_iota(jnp.int32, (L, L), 0)
    cols = lax.broadcasted_iota(jnp.int32, (L, L), 1)
    lower = jnp.where(rows >= cols, 1.0, 0.0)
    sums = lambda value: jnp.dot(lower, value, precision=lax.Precision.HIGHEST, preferred_element_type=F32)
    upper_half = sums(fall[:L])
    cum = jnp.concatenate([upper_half, sums(fall[L:]) + upper_half[L - 1 : L]], axis=0)
    middle = 0.5 * cum[SPAN - 1 : SPAN]
    a_ref[...] = split_high_low(jnp.exp(middle - cum) * dt, heads)
    e_ref[...] = split_high_low(jnp.exp(cum - middle), heads)
    w_ref[...] = split_high_low(wide(skip_ref[...]) / dt, heads)
    em_ref[0] = split_high_low(jnp.broadcast_to(jnp.exp(middle), (16, LANES)), heads)


def fill_conv(buf, held, source, halo_ref, weights_ref, codes, span):
    pieces = source.shape[1] // LANES

    @pl.when(span == 0)
    def _():
        for piece in range(pieces):
            buf[piece, 8 - REACH : 8, :] = halo_ref[:, piece * LANES : (piece + 1) * LANES].astype(F32)

    @pl.when(span > 0)
    def _():
        for piece in range(pieces):
            buf[piece, 0:8, :] = buf[piece, SPAN : SPAN + 8, :]

    weights = 0.5 * weights_ref[...].astype(F32)
    for piece in range(pieces):
        lanes = slice(piece * LANES, (piece + 1) * LANES)
        buf[piece, 8 : 8 + SPAN, :] = source[:, lanes].astype(F32)
        for row in range(0, SPAN, TILE):
            acc = conv_tile(buf, piece, weights[:, lanes], row, TILE, codes[row : row + TILE, :])
            held[row : row + TILE, lanes] = silu_of_half(acc)


def entering_id(ids, k):
    return (jnp.max(ids[k : k + 1]) - 1.0).astype(jnp.int32)


def b_kernel(
    seg_s, b_ref, halo_ref, ids_ref, wb_ref, seg_ref,
    bs_ref, bt_ref, code_ref, info_ref,
    buf, seg_buf, held, *, parts
):
    span = pl.program_id(0)
    ids = ids_ref[...].astype(F32)
    start = span * SPAN
    first = seg_s[start]
    last = seg_s[start + SPAN - 1]
    before = jnp.where(span == 0, entering_id(ids, REACH - 1), seg_s[jnp.maximum(start - 1, 0)])
    oldest = jnp.where(span == 0, entering_id(ids, 0), seg_s[jnp.maximum(start - REACH, 0)])
    cut = (first != last) | ((oldest != first) & (oldest >= 0))
    info_ref[2 * span] = cut.astype(jnp.int32)
    info_ref[2 * span + 1] = (before == last).astype(jnp.int32)

    @pl.when(span == 0)
    def _():
        seg_buf[8 - REACH : 8, :] = ids - 1.0

    @pl.when(span > 0)
    def _():
        seg_buf[0:8, :] = seg_buf[SPAN : SPAN + 8, :]

    seg_row = seg_ref[...].astype(F32)
    seg_buf[8 : 8 + SPAN, :] = jnp.transpose(jnp.broadcast_to(seg_row, (LANES, SPAN)))
    own = seg_buf[8 : 8 + SPAN, :]
    code = jnp.zeros((SPAN, LANES), F32)
    for step in range(1, KCONV):
        code = code + jnp.where(seg_buf[8 - step : 8 - step + SPAN, :] == own, 1.0, 0.0)
    code_ref[...] = code
    fill_conv(buf, held, b_ref, halo_ref, wb_ref, code_ref, span)
    bs_ref[...] = held[...].astype(BF16)
    latest = seg_row == last.astype(F32)
    for g in range(parts):
        bt_ref[g] = jnp.where(latest, jnp.transpose(held[:, g * N : (g + 1) * N]), 0.0).astype(BF16)


def score_kernel(
    seg_s, c_ref, halo_ref, ids_ref, wc_ref, seg_ref, bs_ref, code_ref, token_ref,
    m_ref,
    buf, held, *, parts
):
    del token_ref
    span = pl.program_id(0)
    ids = ids_ref[...].astype(F32)
    start = span * SPAN
    before = jnp.where(span == 0, entering_id(ids, REACH - 1), seg_s[jnp.maximum(start - 1, 0)])
    fill_conv(buf, held, c_ref, halo_ref, wc_ref, code_ref, span)
    halves = [slice(half * L, (half + 1) * L) for half in range(2)]
    seg_rows = [seg_ref[:, half].astype(F32) for half in halves]
    seg_cols = [jnp.transpose(jnp.broadcast_to(seg_row, (L, L))) for seg_row in seg_rows]
    rows = lax.broadcasted_iota(jnp.int32, (L, L), 0)
    cols = lax.broadcasted_iota(jnp.int32, (L, L), 1)
    causal = rows >= cols
    across = (((1,), (1,)), ((), ()))
    for g in range(parts):
        lanes = slice(g * N, (g + 1) * N)
        cs = held[:, lanes].astype(BF16)
        early = lax.dot_general(cs, bs_ref[halves[0], lanes], across, preferred_element_type=F32)
        late = lax.dot_general(cs[L:], bs_ref[halves[1], lanes], across, preferred_element_type=F32)
        allowed = [causal & (seg_cols[half] == seg_rows[half]) for half in range(2)]
        m_ref[g, 0:L, 0:L] = jnp.where(allowed[0], early[:L], 0.0).astype(BF16)
        m_ref[g, L:SPAN, 0:L] = jnp.where(seg_cols[1] == seg_rows[0], early[L:], 0.0).astype(BF16)
        m_ref[g, 0:L, L + N :] = jnp.zeros((L, L), BF16)
        m_ref[g, L:SPAN, L + N :] = jnp.where(allowed[1], late, 0.0).astype(BF16)
        for half in range(2):
            enters = seg_cols[half] == before.astype(F32)
            m_ref[g, halves[half], L : L + N] = jnp.where(enters, held[halves[half], lanes], 0.0).astype(BF16)


def state_kernel(
    info_ref, x_ref, halo_ref, w_ref, bt_ref, a_ref, em_ref, code_ref,
    u_ref, state_ref, first_ref, factor_ref,
    buf, carry, spread, *, first_head, heads
):
    span = pl.program_id(1)
    width = x_ref.shape[1]
    chunks = width // CHUNK
    inner = CHUNK // LANES
    cut = info_ref[2 * span] > 0

    @pl.when(span == 0)
    def _():
        spread_matrix(spread, first_head + pl.program_id(0) * (width // P_SIZE), heads)
        for piece in range(width // LANES):
            buf[piece, 8 - REACH : 8, :] = halo_ref[:, piece * LANES : (piece + 1) * LANES].astype(F32)

    @pl.when(span > 0)
    def _():
        buf[:, 0:8, :] = buf[:, SPAN : SPAN + 8, :]

    def convolve(masked):
        for chunk in range(chunks):
            cols = slice(chunk * CHUNK, (chunk + 1) * CHUNK)
            scale = dot(a_ref[...], spread[:, cols])
            for piece in range(inner):
                index = chunk * inner + piece
                lanes = slice(index * LANES, (index + 1) * LANES)
                weights = 0.5 * w_ref[:, lanes].astype(F32)
                buf[index, 8 : 8 + SPAN, :] = x_ref[:, lanes].astype(F32)
                for row in range(0, SPAN, TILE):
                    code = code_ref[row : row + TILE, :] if masked else None
                    acc = conv_tile(buf, index, weights, row, TILE, code)
                    factor = scale[row : row + TILE, piece * LANES : (piece + 1) * LANES]
                    u_ref[row : row + TILE, lanes] = (silu_of_half(acc) * factor).astype(BF16)
            grown = dot(bt_ref[0], u_ref[:, cols])
            carry[span, :, cols] = grown

    @pl.when(cut)
    def _():
        convolve(True)

    @pl.when(jnp.logical_not(cut))
    def _():
        convolve(False)

    @pl.when(span == 1)
    def _():
        passes = [info_ref[2 * k + 1].astype(F32) for k in range(2)]
        for chunk in range(chunks):
            cols = slice(chunk * CHUNK, (chunk + 1) * CHUNK)
            early, late = (dot(em_ref[k], spread[:, cols])[0:1] for k in range(2))
            middle = early * carry[0, :, cols]
            first_ref[:, cols] = middle.astype(BF16)
            state_ref[:, cols] = (late * carry[1, :, cols] + (passes[1] * late * late) * middle).astype(BF16)
            factor_ref[:, cols] = (passes[0] * passes[1]) * (early * early * late * late)


def final_kernel(
    info_ref, u_ref, gate_ref, m_ref, e_ref, w_ref, em_ref, first_ref, t0_ref, t1_ref, t2_ref, gain_ref,
    out_ref, done_ref,
    enter, spread, held, *, first_head, heads
):
    span = pl.program_id(0)
    width = u_ref.shape[1]
    chunks = width // CHUNK
    strips = [slice(chunk * CHUNK, (chunk + 1) * CHUNK) for chunk in range(chunks)]

    @pl.when(span == 0)
    def _():
        done_ref[...] = jnp.zeros_like(done_ref)
        spread_matrix(spread, first_head, heads)
        passes = info_ref[1].astype(F32)
        for cols in strips:
            early, late = (dot(em_ref[k], spread[:, cols])[0:1] for k in range(2))
            came = t0_ref[:, cols].astype(F32) + t1_ref[:, cols].astype(F32) + t2_ref[:, cols].astype(F32)
            enter[0, :, cols] = (early * came).astype(BF16)
            grown = first_ref[:, cols].astype(F32) + (passes * early * early) * came
            enter[1, :, cols] = (late * grown).astype(BF16)

    squares = [jnp.zeros((L, LANES), F32) for _ in range(2)]
    for cols in strips:
        part = spread[:, cols]
        sources = jnp.concatenate([u_ref[0:L, cols], enter[span, :, cols]], axis=0)
        total = dot(m_ref[0, :, 0 : L + N], sources)
        last = dot(m_ref[0, L:SPAN, L + N :], u_ref[L:SPAN, cols])
        outer = dot(e_ref[...], part)
        direct = dot(w_ref[...], part)
        for half in range(2):
            own = slice(half * L, (half + 1) * L)
            sums = total[own] + direct[own] * u_ref[own, cols].astype(F32)
            if half == 1:
                sums = sums + last
            v = (outer[own] * sums) * silu_of_half(0.5 * gate_ref[own, cols].astype(F32))
            held[own, cols] = v
            v2 = v * v
            for piece in range(CHUNK // LANES):
                squares[half] = squares[half] + v2[:, piece * LANES : (piece + 1) * LANES]
    for half in range(2):
        own = slice(half * L, (half + 1) * L)
        mean = jnp.sum(squares[half], axis=1, keepdims=True) * (1.0 / width)
        scale = lax.rsqrt(mean + 1e-05)
        for cols in strips:
            out_ref[own, cols] = (held[own, cols] * scale * gain_ref[:, cols]).astype(BF16)


def state_after_kernel(*refs, first_head, heads):
    state_kernel(*refs[:8], *refs[10:], first_head=first_head, heads=heads)


def scale_kernel(value_ref, factor_ref, *refs):
    out_ref = refs[-1]
    for row in range(0, N, 64):
        rows = slice(row, row + 64)
        out_ref[rows] = (factor_ref[...] * value_ref[rows].astype(F32)).astype(BF16)


def final_into_kernel(*refs, first_head, heads):
    final_kernel(*refs[:12], *refs[13:], first_head=first_head, heads=heads)


def per_device(
    x_in, gate_in, b_in, c_in, dt_raw, conv_x, conv_b, conv_c, dt_bias, a_log, skip, norm_gain, segment
):
    rows, channels = x_in.shape
    width_bc = b_in.shape[1]
    parts = width_bc // N
    width = channels // parts
    heads = width // P_SIZE
    all_heads = dt_raw.shape[1]
    blocks = rows // L
    spans = rows // SPAN
    assert spans == 2
    devices = lax.axis_size("req")
    step_width = width
    shape = jax.ShapeDtypeStruct
    smem = pl.BlockSpec(memory_space=pltpu.SMEM)
    whole = lambda *_: (0, 0)
    at_row = lambda k, *_: (k, 0)

    def params(axes):
        return pltpu.CompilerParams(dimension_semantics=("arbitrary",) * axes, vmem_limit_bytes=30 << 20)

    def cost(flops, mib):
        return pl.CostEstimate(flops=flops, bytes_accessed=mib << 20, transcendentals=0)

    x_in, b_in, c_in = (pltpu.with_memory_space_constraint(value, pltpu.HBM) for value in (x_in, b_in, c_in))
    shift = [(k, k + 1) for k in range(devices - 1)]
    inside = [(k, k + 1) for k in range(0, devices - 1, 2)]
    across = [(k, k + 1) for k in range(1, devices - 1, 2)]

    last_rows = lambda *_: (rows // 16 - 1, 0)
    tail_width = channels + 2 * width_bc + LANES
    tail = pl.pallas_call(
        tail_kernel,
        grid=(1,),
        in_specs=[
            smem,
            pl.BlockSpec((16, channels), last_rows),
            pl.BlockSpec((16, width_bc), last_rows),
            pl.BlockSpec((16, width_bc), last_rows),
        ],
        out_specs=pl.BlockSpec((REACH, tail_width), whole),
        out_shape=shape((REACH, tail_width), BF16),
        compiler_params=params(1),
        cost_estimate=cost(1000, 0),
        name="tails",
    )(segment, x_in, b_in, c_in)
    halo = lax.ppermute(tail, "req", shift)

    row = lambda value: value.reshape(1, -1)
    narrow = pl.BlockSpec((SPAN, LANES), at_row)
    a_hl, e_hl, w_hl, em = pl.pallas_call(
        decay_kernel,
        grid=(spans,),
        in_specs=[pl.BlockSpec((SPAN, all_heads), at_row)] + [pl.BlockSpec((1, all_heads), whole)] * 3,
        out_specs=[narrow, narrow, narrow, pl.BlockSpec((1, 16, LANES), lambda k: (k, 0, 0))],
        out_shape=[shape((rows, LANES), BF16)] * 3 + [shape((spans, 16, LANES), BF16)],
        compiler_params=params(1),
        cost_estimate=cost(3 * 10**9, 1),
        name="decays",
    )(dt_raw, row(dt_bias), row(a_log), row(skip))

    halo_bc = lambda which: pl.BlockSpec((REACH, width_bc), lambda *_: (0, channels // width_bc + which))
    ids_spec = pl.BlockSpec((REACH, LANES), lambda *_: (0, tail_width // LANES - 1))
    seg_spec = pl.BlockSpec((1, SPAN), lambda k: (0, k))
    wide_bc = pl.BlockSpec((SPAN, width_bc), at_row)
    conv_scratch = [pltpu.VMEM((width_bc // LANES, SPAN + 8, LANES), F32)]
    bs, bt, code, info = pl.pallas_call(
        functools.partial(b_kernel, parts=parts),
        grid=(spans,),
        in_specs=[smem, wide_bc, halo_bc(0), ids_spec, pl.BlockSpec((KCONV, width_bc), whole), seg_spec],
        out_specs=[wide_bc, pl.BlockSpec((parts, N, SPAN), lambda k: (0, 0, k)), narrow, smem],
        out_shape=[
            shape((rows, width_bc), BF16),
            shape((parts, N, rows), BF16),
            shape((rows, LANES), F32),
            shape((2 * spans,), jnp.int32),
        ],
        scratch_shapes=conv_scratch + [pltpu.VMEM((SPAN + 8, LANES), F32), pltpu.VMEM((SPAN, width_bc), F32)],
        compiler_params=params(1),
        cost_estimate=cost(10**9, 3),
        name="b_rows",
    )(segment, b_in, halo, halo, conv_b, row(segment))

    def score(token):
        return pl.pallas_call(
            functools.partial(score_kernel, parts=parts),
            grid=(spans,),
            in_specs=[
                smem, wide_bc, halo_bc(1), ids_spec, pl.BlockSpec((KCONV, width_bc), whole), seg_spec, wide_bc, narrow,
                pl.BlockSpec(memory_space=pl.ANY),
            ],
            out_specs=pl.BlockSpec((parts, SPAN, N + SPAN), lambda k: (0, k, 0)),
            out_shape=shape((parts, rows, N + SPAN), BF16),
            scratch_shapes=conv_scratch + [pltpu.VMEM((SPAN, width_bc), F32)],
            compiler_params=params(1),
            cost_estimate=cost(3 * 10**9, 4),
            name="scores",
        )(segment, c_in, halo, halo, conv_c, row(segment), bs, code, token)

    em_spec = lambda: pl.BlockSpec((spans, 16, LANES), lambda *_: (0, 0, 0))

    anywhere = pl.BlockSpec(memory_space=pl.ANY)

    def local(g, tokens):
        steps = width // step_width
        at_cols = lambda j, k: (0, g * steps + j)
        return pl.pallas_call(
            functools.partial(state_after_kernel if tokens else state_kernel, first_head=g * heads, heads=all_heads),
            grid=(steps, spans),
            in_specs=[
                smem,
                pl.BlockSpec((SPAN, step_width), lambda j, k: (k, g * steps + j)),
                pl.BlockSpec((REACH, step_width), at_cols),
                pl.BlockSpec((KCONV, step_width), at_cols),
                pl.BlockSpec((1, N, SPAN), lambda j, k: (g, 0, k)),
                pl.BlockSpec((SPAN, LANES), lambda j, k: (k, 0)),
                em_spec(),
                pl.BlockSpec((SPAN, LANES), lambda j, k: (k, 0)),
            ]
            + [anywhere] * len(tokens),
            out_specs=[
                pl.BlockSpec((SPAN, step_width), lambda j, k: (k, j)),
                pl.BlockSpec((N, step_width), lambda j, k: (0, j)),
                pl.BlockSpec((N, step_width), lambda j, k: (0, j)),
                pl.BlockSpec((1, step_width), lambda j, k: (0, j)),
            ],
            out_shape=[
                shape((rows, width), BF16),
                shape((N, width), BF16),
                shape((N, width), BF16),
                shape((1, width), F32),
            ],
            scratch_shapes=[
                pltpu.VMEM((step_width // LANES, SPAN + 8, LANES), F32),
                pltpu.VMEM((spans, N, step_width), F32),
                pltpu.VMEM((LANES, step_width), BF16),
            ],
            compiler_params=params(2),
            cost_estimate=cost(6 * 10**9, 10),
            name="state",
        )(info, x_in, halo, conv_x, bt, a_hl, em, code, *tokens)

    def scaled(value, factor, token):
        tokens = [] if token is None else [token]
        whole_spec = lambda array: pl.BlockSpec(array.shape, whole)
        return pl.pallas_call(
            scale_kernel,
            grid=(1,),
            in_specs=[whole_spec(value), whole_spec(factor)] + [anywhere] * len(tokens),
            out_specs=whole_spec(value),
            out_shape=shape(value.shape, BF16),
            compiler_params=params(1),
            cost_estimate=cost(10**6, 2),
            name="scale",
        )(value, factor, *tokens)

    def leave(state, first, factor):
        return (state.astype(F32) + factor * first.astype(F32)).astype(BF16)

    def travel(state, first, leaving, factor, token):
        entering, passed = jnp.zeros_like(state), jnp.zeros_like(state)
        rounds = devices // 2 - 1
        for turn in range(rounds):
            entering = lax.ppermute(leaving, "req", across)
            passed = lax.ppermute(scaled(entering, factor, token), "req", inside)
            if turn < rounds - 1:
                leaving = leave(state, first.astype(F32) + passed.astype(F32), factor)
        return first, entering, passed

    def final(g, u, m, first, carries, out):
        at_group = lambda *_: (0, g)
        own = pl.BlockSpec((SPAN, width), lambda k: (k, g))
        square = pl.BlockSpec((N, width), whole)
        in_specs = [
            smem,
            pl.BlockSpec((SPAN, width), at_row),
            own,
            pl.BlockSpec((1, SPAN, N + SPAN), lambda k: (g, k, 0)),
            narrow,
            narrow,
            em_spec(),
            square,
            square,
            square,
            square,
            pl.BlockSpec((1, width), at_group),
        ]
        operands = [info, u, gate_in, m, e_hl, w_hl, em, first, *carries, row(norm_gain)]
        if out is not None:
            in_specs.append(anywhere)
            operands.append(out)
        return pl.pallas_call(
            functools.partial(final_kernel if out is None else final_into_kernel, first_head=g * heads, heads=all_heads),
            grid=(spans,),
            in_specs=in_specs,
            out_specs=[own, pl.BlockSpec((8, LANES), whole)],
            out_shape=[shape((rows, channels), BF16), shape((8, LANES), F32)],
            scratch_shapes=[
                pltpu.VMEM((spans, N, width), BF16),
                pltpu.VMEM((LANES, width), BF16),
                pltpu.VMEM((SPAN, width), F32),
            ],
            input_output_aliases={} if out is None else {12: 0},
            compiler_params=params(1),
            cost_estimate=cost(6 * 10**9, 16),
            name="final",
        )(*operands)

    leaving, locals_, m = None, [], None
    for g in range(parts):
        u, state, inner, factor = local(g, [leaving, m] if g else [])
        first = lax.ppermute(state, "req", inside)
        if m is None:
            m = score(factor)
        leaving = leave(state, first, factor)
        locals_.append((u, inner, state, first, leaving, factor))
    out = done = None
    for g in range(parts):
        u, inner, *sent = locals_[g]
        out, done = final(g, u, m, inner, travel(*sent, done), out)
    return out


def solution(mesh):
    rows = P(("groups", "req"), "tp")
    placed = (rows,) * 5 + (P(None, "tp"),) * 3 + (P("tp"),) * 4 + (P(("groups", "req")),)
    return jax.shard_map(
        per_device,
        mesh=mesh,
        in_specs=placed,
        out_specs=rows,
        check_vma=False,
    )
```

```python
import functools

import jax
import jax.numpy as jnp
from jax import lax
from jax.experimental import pallas as pl
from jax.experimental.pallas import tpu as pltpu
from jax.sharding import PartitionSpec as P

P_SIZE = 64
N = 256
L = 256
SPAN = 2 * L
KCONV = 4
REACH = KCONV - 1
LANES = 128
CHUNK = 256
TILE = 128
F32 = jnp.float32
BF16 = jnp.bfloat16


def dot(a, b):
    return jnp.dot(a, b, preferred_element_type=F32)


def split_high_low(value, heads):
    lane = lax.broadcasted_iota(jnp.int32, value.shape, 1)
    high = value.astype(BF16).astype(F32)
    low = jnp.where(lane < 2 * heads, value - high, 0.0)
    return jnp.where(lane < heads, high, low).astype(BF16)


def silu_of_half(half):
    return half + half * jnp.tanh(half)


def spread_matrix(ref, first_head, heads):
    width = ref.shape[1]
    rows = lax.broadcasted_iota(jnp.int32, (LANES, width), 0) & (heads - 1)
    cols = lax.broadcasted_iota(jnp.int32, (LANES, width), 1) >> 6
    ref[...] = jnp.where(rows == cols + first_head, 1.0, 0.0).astype(BF16)


def conv_tile(buf, index, weights, row, rows, code):
    acc = None
    for step in range(KCONV):
        term = buf[index, pl.ds(8 - step + row, rows), :] * weights[REACH - step : KCONV - step]
        if code is not None and step > 0:
            term = jnp.where(code >= step, term, 0.0)
        acc = term if acc is None else acc + term
    return acc


def tail_kernel(seg_s, x_ref, b_ref, c_ref, out_ref):
    rows = seg_s.shape[0]
    start = 0
    for ref in (x_ref, b_ref, c_ref):
        width = ref.shape[1]
        value = ref[...].astype(F32)
        out_ref[:, start : start + width] = value[16 - REACH :].astype(BF16)
        start += width
    ids = [jnp.full((1, LANES), seg_s[rows - REACH + k] + 1, jnp.int32).astype(F32) for k in range(REACH)]
    out_ref[:, start:] = jnp.concatenate(ids, axis=0).astype(BF16)


def decay_kernel(dt_ref, bias_ref, a_log_ref, skip_ref, a_ref, e_ref, w_ref, em_ref):
    heads = dt_ref.shape[1]
    copies = LANES // heads
    wide = lambda value: jnp.concatenate([value] * copies, axis=1)
    z = wide(dt_ref[...].astype(F32)) + wide(bias_ref[...])
    dt = jnp.maximum(z, 0.0) + jnp.log1p(jnp.exp(-jnp.abs(z)))
    fall = -dt * wide(jnp.exp(a_log_ref[...]))
    rows = lax.broadcasted_iota(jnp.int32, (L, L), 0)
    cols = lax.broadcasted_iota(jnp.int32, (L, L), 1)
    lower = jnp.where(rows >= cols, 1.0, 0.0)
    sums = lambda value: jnp.dot(lower, value, precision=lax.Precision.HIGHEST, preferred_element_type=F32)
    upper_half = sums(fall[:L])
    cum = jnp.concatenate([upper_half, sums(fall[L:]) + upper_half[L - 1 : L]], axis=0)
    middle = 0.5 * cum[SPAN - 1 : SPAN]
    a_ref[...] = split_high_low(jnp.exp(middle - cum) * dt, heads)
    e_ref[...] = split_high_low(jnp.exp(cum - middle), heads)
    w_ref[...] = split_high_low(wide(skip_ref[...]) / dt, heads)
    em_ref[0] = split_high_low(jnp.broadcast_to(jnp.exp(middle), (16, LANES)), heads)


def fill_conv(buf, held, source, halo_ref, weights_ref, codes, span):
    pieces = source.shape[1] // LANES

    @pl.when(span == 0)
    def _():
        for piece in range(pieces):
            buf[piece, 8 - REACH : 8, :] = halo_ref[:, piece * LANES : (piece + 1) * LANES].astype(F32)

    @pl.when(span > 0)
    def _():
        for piece in range(pieces):
            buf[piece, 0:8, :] = buf[piece, SPAN : SPAN + 8, :]

    weights = 0.5 * weights_ref[...].astype(F32)
    for piece in range(pieces):
        lanes = slice(piece * LANES, (piece + 1) * LANES)
        buf[piece, 8 : 8 + SPAN, :] = source[:, lanes].astype(F32)
        for row in range(0, SPAN, TILE):
            acc = conv_tile(buf, piece, weights[:, lanes], row, TILE, codes[row : row + TILE, :])
            held[row : row + TILE, lanes] = silu_of_half(acc)


def entering_id(ids, k):
    return (jnp.max(ids[k : k + 1]) - 1.0).astype(jnp.int32)


def b_kernel(
    seg_s, b_ref, halo_ref, ids_ref, wb_ref, seg_ref,
    bs_ref, bt_ref, code_ref, info_ref,
    buf, seg_buf, held, *, parts
):
    span = pl.program_id(0)
    ids = ids_ref[...].astype(F32)
    start = span * SPAN
    first = seg_s[start]
    last = seg_s[start + SPAN - 1]
    before = jnp.where(span == 0, entering_id(ids, REACH - 1), seg_s[jnp.maximum(start - 1, 0)])
    oldest = jnp.where(span == 0, entering_id(ids, 0), seg_s[jnp.maximum(start - REACH, 0)])
    cut = (first != last) | ((oldest != first) & (oldest >= 0))
    info_ref[2 * span] = cut.astype(jnp.int32)
    info_ref[2 * span + 1] = (before == last).astype(jnp.int32)

    @pl.when(span == 0)
    def _():
        seg_buf[8 - REACH : 8, :] = ids - 1.0

    @pl.when(span > 0)
    def _():
        seg_buf[0:8, :] = seg_buf[SPAN : SPAN + 8, :]

    seg_row = seg_ref[...].astype(F32)
    seg_buf[8 : 8 + SPAN, :] = jnp.transpose(jnp.broadcast_to(seg_row, (LANES, SPAN)))
    own = seg_buf[8 : 8 + SPAN, :]
    code = jnp.zeros((SPAN, LANES), F32)
    for step in range(1, KCONV):
        code = code + jnp.where(seg_buf[8 - step : 8 - step + SPAN, :] == own, 1.0, 0.0)
    code_ref[...] = code
    fill_conv(buf, held, b_ref, halo_ref, wb_ref, code_ref, span)
    bs_ref[...] = held[...].astype(BF16)
    latest = jnp.where(seg_row == last.astype(F32), 1.0, 0.0).astype(BF16)
    for g in range(parts):
        bt_ref[g] = jnp.transpose(bs_ref[:, g * N : (g + 1) * N]) * latest


def score_kernel(
    seg_s, c_ref, halo_ref, ids_ref, wc_ref, seg_ref, bs_ref, code_ref, token_ref,
    m_ref,
    buf, held, *, parts
):
    del token_ref
    span = pl.program_id(0)
    ids = ids_ref[...].astype(F32)
    start = span * SPAN
    before = jnp.where(span == 0, entering_id(ids, REACH - 1), seg_s[jnp.maximum(start - 1, 0)])
    fill_conv(buf, held, c_ref, halo_ref, wc_ref, code_ref, span)
    halves = [slice(half * L, (half + 1) * L) for half in range(2)]
    seg_rows = [seg_ref[:, half].astype(F32) for half in halves]
    seg_cols = [jnp.transpose(jnp.broadcast_to(seg_row, (L, L))) for seg_row in seg_rows]
    rows = lax.broadcasted_iota(jnp.int32, (L, L), 0)
    cols = lax.broadcasted_iota(jnp.int32, (L, L), 1)
    causal = rows >= cols
    across = (((1,), (1,)), ((), ()))
    for g in range(parts):
        lanes = slice(g * N, (g + 1) * N)
        cs = held[:, lanes].astype(BF16)
        early = lax.dot_general(cs, bs_ref[halves[0], lanes], across, preferred_element_type=F32)
        late = lax.dot_general(cs[L:], bs_ref[halves[1], lanes], across, preferred_element_type=F32)
        allowed = [causal & (seg_cols[half] == seg_rows[half]) for half in range(2)]
        m_ref[g, 0:L, 0:L] = jnp.where(allowed[0], early[:L], 0.0).astype(BF16)
        m_ref[g, L:SPAN, 0:L] = jnp.where(seg_cols[1] == seg_rows[0], early[L:], 0.0).astype(BF16)
        m_ref[g, 0:L, L + N :] = jnp.zeros((L, L), BF16)
        m_ref[g, L:SPAN, L + N :] = jnp.where(allowed[1], late, 0.0).astype(BF16)
        for half in range(2):
            enters = seg_cols[half] == before.astype(F32)
            m_ref[g, halves[half], L : L + N] = jnp.where(enters, held[halves[half], lanes], 0.0).astype(BF16)


def state_kernel(
    info_ref, x_ref, halo_ref, w_ref, bt_ref, a_ref, em_ref, code_ref,
    u_ref, state_ref, first_ref, factor_ref,
    buf, carry, spread, *, first_head, heads
):
    span = pl.program_id(1)
    width = x_ref.shape[1]
    chunks = width // CHUNK
    inner = CHUNK // LANES
    cut = info_ref[2 * span] > 0

    @pl.when(span == 0)
    def _():
        spread_matrix(spread, first_head + pl.program_id(0) * (width // P_SIZE), heads)
        for piece in range(width // LANES):
            buf[piece, 8 - REACH : 8, :] = halo_ref[:, piece * LANES : (piece + 1) * LANES].astype(F32)

    @pl.when(span > 0)
    def _():
        buf[:, 0:8, :] = buf[:, SPAN : SPAN + 8, :]

    def convolve(masked):
        for chunk in range(chunks):
            cols = slice(chunk * CHUNK, (chunk + 1) * CHUNK)
            scale = dot(a_ref[...], spread[:, cols])
            for piece in range(inner):
                index = chunk * inner + piece
                lanes = slice(index * LANES, (index + 1) * LANES)
                weights = 0.5 * w_ref[:, lanes].astype(F32)
                buf[index, 8 : 8 + SPAN, :] = x_ref[:, lanes].astype(F32)
                for row in range(0, SPAN, TILE):
                    code = code_ref[row : row + TILE, :] if masked else None
                    acc = conv_tile(buf, index, weights, row, TILE, code)
                    factor = scale[row : row + TILE, piece * LANES : (piece + 1) * LANES]
                    u_ref[row : row + TILE, lanes] = (silu_of_half(acc) * factor).astype(BF16)
            grown = dot(bt_ref[0], u_ref[:, cols])
            carry[span, :, cols] = grown

    @pl.when(cut)
    def _():
        convolve(True)

    @pl.when(jnp.logical_not(cut))
    def _():
        convolve(False)

    @pl.when(span == 1)
    def _():
        passes = [info_ref[2 * k + 1].astype(F32) for k in range(2)]
        for chunk in range(chunks):
            cols = slice(chunk * CHUNK, (chunk + 1) * CHUNK)
            early, late = (dot(em_ref[k], spread[:, cols])[0:1] for k in range(2))
            middle = early * carry[0, :, cols]
            first_ref[:, cols] = middle.astype(BF16)
            state_ref[:, cols] = (late * carry[1, :, cols] + (passes[1] * late * late) * middle).astype(BF16)
            factor_ref[:, cols] = (passes[0] * passes[1]) * (early * early * late * late)


def final_kernel(
    info_ref, u_ref, gate_ref, m_ref, e_ref, w_ref, em_ref, first_ref, t0_ref, t1_ref, t2_ref, gain_ref,
    out_ref, done_ref,
    enter, spread, held, *, first_head, heads
):
    span = pl.program_id(0)
    width = u_ref.shape[1]
    chunks = width // CHUNK
    strips = [slice(chunk * CHUNK, (chunk + 1) * CHUNK) for chunk in range(chunks)]

    @pl.when(span == 0)
    def _():
        done_ref[...] = jnp.zeros_like(done_ref)
        spread_matrix(spread, first_head, heads)
        passes = info_ref[1].astype(F32)
        for cols in strips:
            early, late = (dot(em_ref[k], spread[:, cols])[0:1] for k in range(2))
            came = t0_ref[:, cols].astype(F32) + t1_ref[:, cols].astype(F32) + t2_ref[:, cols].astype(F32)
            enter[0, :, cols] = (early * came).astype(BF16)
            grown = first_ref[:, cols].astype(F32) + (passes * early * early) * came
            enter[1, :, cols] = (late * grown).astype(BF16)

    squares = [jnp.zeros((L, LANES), F32) for _ in range(2)]
    for cols in strips:
        part = spread[:, cols]
        sources = jnp.concatenate([u_ref[0:L, cols], enter[span, :, cols]], axis=0)
        total = dot(m_ref[0, :, 0 : L + N], sources)
        last = dot(m_ref[0, L:SPAN, L + N :], u_ref[L:SPAN, cols])
        outer = dot(e_ref[...], part)
        direct = dot(w_ref[...], part)
        for half in range(2):
            own = slice(half * L, (half + 1) * L)
            sums = total[own] + direct[own] * u_ref[own, cols].astype(F32)
            if half == 1:
                sums = sums + last
            v = (outer[own] * sums) * silu_of_half(0.5 * gate_ref[own, cols].astype(F32))
            held[own, cols] = v
            v2 = v * v
            for piece in range(CHUNK // LANES):
                squares[half] = squares[half] + v2[:, piece * LANES : (piece + 1) * LANES]
    for half in range(2):
        own = slice(half * L, (half + 1) * L)
        mean = jnp.sum(squares[half], axis=1, keepdims=True) * (1.0 / width)
        scale = lax.rsqrt(mean + 1e-05)
        for cols in strips:
            out_ref[own, cols] = (held[own, cols] * scale * gain_ref[:, cols]).astype(BF16)


def state_after_kernel(*refs, first_head, heads):
    state_kernel(*refs[:8], *refs[9:], first_head=first_head, heads=heads)


def scale_kernel(value_ref, factor_ref, *refs):
    out_ref = refs[-1]
    for row in range(0, N, 64):
        rows = slice(row, row + 64)
        out_ref[rows] = (factor_ref[...] * value_ref[rows].astype(F32)).astype(BF16)


def final_into_kernel(*refs, first_head, heads):
    final_kernel(*refs[:12], *refs[13:], first_head=first_head, heads=heads)


def per_device(
    x_in, gate_in, b_in, c_in, dt_raw, conv_x, conv_b, conv_c, dt_bias, a_log, skip, norm_gain, segment
):
    rows, channels = x_in.shape
    width_bc = b_in.shape[1]
    parts = width_bc // N
    width = channels // parts
    heads = width // P_SIZE
    all_heads = dt_raw.shape[1]
    blocks = rows // L
    spans = rows // SPAN
    assert spans == 2
    devices = lax.axis_size("req")
    step_width = width
    shape = jax.ShapeDtypeStruct
    smem = pl.BlockSpec(memory_space=pltpu.SMEM)
    whole = lambda *_: (0, 0)
    at_row = lambda k, *_: (k, 0)

    def params(axes, mib=16):
        return pltpu.CompilerParams(dimension_semantics=("arbitrary",) * axes, vmem_limit_bytes=mib << 20)

    def cost(flops, mib):
        return pl.CostEstimate(flops=flops, bytes_accessed=mib << 20, transcendentals=0)

    x_in, b_in, c_in = (pltpu.with_memory_space_constraint(value, pltpu.HBM) for value in (x_in, b_in, c_in))
    shift = [(k, k + 1) for k in range(devices - 1)]
    inside = [(k, k + 1) for k in range(0, devices - 1, 2)]
    across = [(k, k + 1) for k in range(1, devices - 1, 2)]

    last_rows = lambda *_: (rows // 16 - 1, 0)
    tail_width = channels + 2 * width_bc + LANES
    tail = pl.pallas_call(
        tail_kernel,
        grid=(1,),
        in_specs=[
            smem,
            pl.BlockSpec((16, channels), last_rows),
            pl.BlockSpec((16, width_bc), last_rows),
            pl.BlockSpec((16, width_bc), last_rows),
        ],
        out_specs=pl.BlockSpec((REACH, tail_width), whole),
        out_shape=shape((REACH, tail_width), BF16),
        compiler_params=params(1),
        cost_estimate=cost(1000, 0),
        name="tails",
    )(segment, x_in, b_in, c_in)
    halo = lax.ppermute(tail, "req", shift)

    row = lambda value: value.reshape(1, -1)
    narrow = pl.BlockSpec((SPAN, LANES), at_row)
    a_hl, e_hl, w_hl, em = pl.pallas_call(
        decay_kernel,
        grid=(spans,),
        in_specs=[pl.BlockSpec((SPAN, all_heads), at_row)] + [pl.BlockSpec((1, all_heads), whole)] * 3,
        out_specs=[narrow, narrow, narrow, pl.BlockSpec((1, 16, LANES), lambda k: (k, 0, 0))],
        out_shape=[shape((rows, LANES), BF16)] * 3 + [shape((spans, 16, LANES), BF16)],
        compiler_params=params(1),
        cost_estimate=cost(3 * 10**9, 1),
        name="decays",
    )(dt_raw, row(dt_bias), row(a_log), row(skip))

    halo_bc = lambda which: pl.BlockSpec((REACH, width_bc), lambda *_: (0, channels // width_bc + which))
    ids_spec = pl.BlockSpec((REACH, LANES), lambda *_: (0, tail_width // LANES - 1))
    seg_spec = pl.BlockSpec((1, SPAN), lambda k: (0, k))
    wide_bc = pl.BlockSpec((SPAN, width_bc), at_row)
    conv_scratch = [pltpu.VMEM((width_bc // LANES, SPAN + 8, LANES), F32)]
    bs, bt, code, info = pl.pallas_call(
        functools.partial(b_kernel, parts=parts),
        grid=(spans,),
        in_specs=[smem, wide_bc, halo_bc(0), ids_spec, pl.BlockSpec((KCONV, width_bc), whole), seg_spec],
        out_specs=[wide_bc, pl.BlockSpec((parts, N, SPAN), lambda k: (0, 0, k)), narrow, smem],
        out_shape=[
            shape((rows, width_bc), BF16),
            shape((parts, N, rows), BF16),
            shape((rows, LANES), F32),
            shape((2 * spans,), jnp.int32),
        ],
        scratch_shapes=conv_scratch + [pltpu.VMEM((SPAN + 8, LANES), F32), pltpu.VMEM((SPAN, width_bc), F32)],
        compiler_params=params(1),
        cost_estimate=cost(10**9, 3),
        name="b_rows",
    )(segment, b_in, halo, halo, conv_b, row(segment))

    def score(token):
        return pl.pallas_call(
            functools.partial(score_kernel, parts=parts),
            grid=(spans,),
            in_specs=[
                smem, wide_bc, halo_bc(1), ids_spec, pl.BlockSpec((KCONV, width_bc), whole), seg_spec, wide_bc, narrow,
                pl.BlockSpec(memory_space=pl.ANY),
            ],
            out_specs=pl.BlockSpec((parts, SPAN, N + SPAN), lambda k: (0, k, 0)),
            out_shape=shape((parts, rows, N + SPAN), BF16),
            scratch_shapes=conv_scratch + [pltpu.VMEM((SPAN, width_bc), F32)],
            compiler_params=params(1),
            cost_estimate=cost(3 * 10**9, 4),
            name="scores",
        )(segment, c_in, halo, halo, conv_c, row(segment), bs, code, token)

    em_spec = lambda: pl.BlockSpec((spans, 16, LANES), lambda *_: (0, 0, 0))

    anywhere = pl.BlockSpec(memory_space=pl.ANY)

    def local(g, tokens):
        steps = width // step_width
        at_cols = lambda j, k: (0, g * steps + j)
        return pl.pallas_call(
            functools.partial(state_after_kernel if tokens else state_kernel, first_head=g * heads, heads=all_heads),
            grid=(steps, spans),
            in_specs=[
                smem,
                pl.BlockSpec((SPAN, step_width), lambda j, k: (k, g * steps + j)),
                pl.BlockSpec((REACH, step_width), at_cols),
                pl.BlockSpec((KCONV, step_width), at_cols),
                pl.BlockSpec((1, N, SPAN), lambda j, k: (g, 0, k)),
                pl.BlockSpec((SPAN, LANES), lambda j, k: (k, 0)),
                em_spec(),
                pl.BlockSpec((SPAN, LANES), lambda j, k: (k, 0)),
            ]
            + [anywhere] * len(tokens),
            out_specs=[
                pl.BlockSpec((SPAN, step_width), lambda j, k: (k, j)),
                pl.BlockSpec((N, step_width), lambda j, k: (0, j)),
                pl.BlockSpec((N, step_width), lambda j, k: (0, j)),
                pl.BlockSpec((1, step_width), lambda j, k: (0, j)),
            ],
            out_shape=[
                shape((rows, width), BF16),
                shape((N, width), BF16),
                shape((N, width), BF16),
                shape((1, width), F32),
            ],
            scratch_shapes=[
                pltpu.VMEM((step_width // LANES, SPAN + 8, LANES), F32),
                pltpu.VMEM((spans, N, step_width), F32),
                pltpu.VMEM((LANES, step_width), BF16),
            ],
            compiler_params=params(2, 24),
            cost_estimate=cost(6 * 10**9, 10),
            name="state",
        )(info, x_in, halo, conv_x, bt, a_hl, em, code, *tokens)

    def scaled(value, factor, token):
        tokens = [] if token is None else [token]
        whole_spec = lambda array: pl.BlockSpec(array.shape, whole)
        return pl.pallas_call(
            scale_kernel,
            grid=(1,),
            in_specs=[whole_spec(value), whole_spec(factor)] + [anywhere] * len(tokens),
            out_specs=whole_spec(value),
            out_shape=shape(value.shape, BF16),
            compiler_params=params(1),
            cost_estimate=cost(10**6, 2),
            name="scale",
        )(value, factor, *tokens)

    def leave(state, first, factor):
        return (state.astype(F32) + factor * first.astype(F32)).astype(BF16)

    def travel(state, first, leaving, factor, token):
        entering, passed = jnp.zeros_like(state), jnp.zeros_like(state)
        rounds = devices // 2 - 1
        for turn in range(rounds):
            entering = lax.ppermute(leaving, "req", across)
            passed = lax.ppermute(scaled(entering, factor, token), "req", inside[1:])
            if turn < rounds - 1:
                leaving = leave(state, first.astype(F32) + passed.astype(F32), factor)
        return first, entering, passed

    def final(g, u, m, first, carries, out):
        at_group = lambda *_: (0, g)
        own = pl.BlockSpec((SPAN, width), lambda k: (k, g))
        square = pl.BlockSpec((N, width), whole, pipeline_mode=pl.Buffered(1))
        in_specs = [
            smem,
            pl.BlockSpec((SPAN, width), at_row),
            own,
            pl.BlockSpec((1, SPAN, N + SPAN), lambda k: (g, k, 0)),
            narrow,
            narrow,
            em_spec(),
            square,
            square,
            square,
            square,
            pl.BlockSpec((1, width), at_group),
        ]
        operands = [info, u, gate_in, m, e_hl, w_hl, em, first, *carries, row(norm_gain)]
        if out is not None:
            in_specs.append(anywhere)
            operands.append(out)
        return pl.pallas_call(
            functools.partial(final_kernel if out is None else final_into_kernel, first_head=g * heads, heads=all_heads),
            grid=(spans,),
            in_specs=in_specs,
            out_specs=[own, pl.BlockSpec((8, LANES), whole)],
            out_shape=[shape((rows, channels), BF16), shape((8, LANES), F32)],
            scratch_shapes=[
                pltpu.VMEM((spans, N, width), BF16),
                pltpu.VMEM((LANES, width), BF16),
                pltpu.VMEM((SPAN, width), F32),
            ],
            input_output_aliases={} if out is None else {12: 0},
            compiler_params=params(1, 26),
            cost_estimate=cost(6 * 10**9, 16),
            name="final",
        )(*operands)

    leaving, locals_, m = None, [], None
    for g in range(parts):
        u, state, inner, factor = local(g, [leaving] if g else [])
        first = lax.ppermute(state, "req", inside)
        leaving = leave(state, first, factor)
        locals_.append((u, inner, state, first, leaving, factor))
    m = score(factor)
    out = done = None
    for g in range(parts):
        u, inner, *sent = locals_[g]
        out, done = final(g, u, m, inner, travel(*sent, done), out)
    return out


def solution(mesh):
    rows = P(("groups", "req"), "tp")
    placed = (rows,) * 5 + (P(None, "tp"),) * 3 + (P("tp"),) * 4 + (P(("groups", "req")),)
    return jax.shard_map(
        per_device,
        mesh=mesh,
        in_specs=placed,
        out_specs=rows,
        check_vma=False,
    )
```

```python
import functools

import jax
import jax.numpy as jnp
from jax import lax
from jax.experimental import pallas as pl
from jax.experimental.pallas import tpu as pltpu
from jax.sharding import PartitionSpec as P

P_SIZE = 64
N = 256
L = 256
SPAN = 2 * L
KCONV = 4
REACH = KCONV - 1
LANES = 128
CHUNK = 256
TILE = 128
F32 = jnp.float32
BF16 = jnp.bfloat16


def dot(a, b):
    return jnp.dot(a, b, preferred_element_type=F32)


def split_high_low(value, heads):
    lane = lax.broadcasted_iota(jnp.int32, value.shape, 1)
    high = value.astype(BF16).astype(F32)
    low = jnp.where(lane < 2 * heads, value - high, 0.0)
    return jnp.where(lane < heads, high, low).astype(BF16)


def silu_of_half(half):
    return half + half * jnp.tanh(half)


def spread_matrix(ref, first_head, heads):
    width = ref.shape[1]
    rows = lax.broadcasted_iota(jnp.int32, (LANES, width), 0) & (heads - 1)
    cols = lax.broadcasted_iota(jnp.int32, (LANES, width), 1) >> 6
    ref[...] = jnp.where(rows == cols + first_head, 1.0, 0.0).astype(BF16)


def conv_tile(buf, index, weights, row, rows, code):
    acc = None
    for step in range(KCONV):
        term = buf[index, pl.ds(8 - step + row, rows), :] * weights[REACH - step : KCONV - step]
        if code is not None and step > 0:
            term = jnp.where(code >= step, term, 0.0)
        acc = term if acc is None else acc + term
    return acc


def tail_kernel(seg_s, x_ref, b_ref, c_ref, out_ref):
    rows = seg_s.shape[0]
    start = 0
    for ref in (x_ref, b_ref, c_ref):
        width = ref.shape[1]
        value = ref[...].astype(F32)
        out_ref[:, start : start + width] = value[16 - REACH :].astype(BF16)
        start += width
    ids = [jnp.full((1, LANES), seg_s[rows - REACH + k] + 1, jnp.int32).astype(F32) for k in range(REACH)]
    out_ref[:, start:] = jnp.concatenate(ids, axis=0).astype(BF16)


def decay_kernel(dt_ref, bias_ref, a_log_ref, skip_ref, a_ref, e_ref, w_ref, em_ref):
    heads = dt_ref.shape[1]
    copies = LANES // heads
    wide = lambda value: jnp.concatenate([value] * copies, axis=1)
    z = wide(dt_ref[...].astype(F32)) + wide(bias_ref[...])
    dt = jnp.maximum(z, 0.0) + jnp.log1p(jnp.exp(-jnp.abs(z)))
    fall = -dt * wide(jnp.exp(a_log_ref[...]))
    rows = lax.broadcasted_iota(jnp.int32, (L, L), 0)
    cols = lax.broadcasted_iota(jnp.int32, (L, L), 1)
    lower = jnp.where(rows >= cols, 1.0, 0.0)
    sums = lambda value: jnp.dot(lower, value, precision=lax.Precision.HIGHEST, preferred_element_type=F32)
    upper_half = sums(fall[:L])
    cum = jnp.concatenate([upper_half, sums(fall[L:]) + upper_half[L - 1 : L]], axis=0)
    middle = 0.5 * cum[SPAN - 1 : SPAN]
    a_ref[...] = split_high_low(jnp.exp(middle - cum) * dt, heads)
    e_ref[...] = split_high_low(jnp.exp(cum - middle), heads)
    w_ref[...] = split_high_low(wide(skip_ref[...]) / dt, heads)
    em_ref[0] = split_high_low(jnp.broadcast_to(jnp.exp(middle), (16, LANES)), heads)


def fill_conv(buf, held, source, halo_ref, weights_ref, codes, span):
    pieces = source.shape[1] // LANES

    @pl.when(span == 0)
    def _():
        for piece in range(pieces):
            buf[piece, 8 - REACH : 8, :] = halo_ref[:, piece * LANES : (piece + 1) * LANES].astype(F32)

    @pl.when(span > 0)
    def _():
        for piece in range(pieces):
            buf[piece, 0:8, :] = buf[piece, SPAN : SPAN + 8, :]

    weights = 0.5 * weights_ref[...].astype(F32)
    for piece in range(pieces):
        lanes = slice(piece * LANES, (piece + 1) * LANES)
        buf[piece, 8 : 8 + SPAN, :] = source[:, lanes].astype(F32)
        for row in range(0, SPAN, TILE):
            acc = conv_tile(buf, piece, weights[:, lanes], row, TILE, codes[row : row + TILE, :])
            held[row : row + TILE, lanes] = silu_of_half(acc)


def entering_id(ids, k):
    return (jnp.max(ids[k : k + 1]) - 1.0).astype(jnp.int32)


def b_kernel(
    seg_s, b_ref, halo_ref, ids_ref, wb_ref, seg_ref,
    bs_ref, bt_ref, code_ref, info_ref,
    buf, seg_buf, held, *, parts
):
    span = pl.program_id(0)
    ids = ids_ref[...].astype(F32)
    start = span * SPAN
    first = seg_s[start]
    last = seg_s[start + SPAN - 1]
    before = jnp.where(span == 0, entering_id(ids, REACH - 1), seg_s[jnp.maximum(start - 1, 0)])
    oldest = jnp.where(span == 0, entering_id(ids, 0), seg_s[jnp.maximum(start - REACH, 0)])
    cut = (first != last) | ((oldest != first) & (oldest >= 0))
    info_ref[2 * span] = cut.astype(jnp.int32)
    info_ref[2 * span + 1] = (before == last).astype(jnp.int32)

    @pl.when(span == 0)
    def _():
        seg_buf[8 - REACH : 8, :] = ids - 1.0

    @pl.when(span > 0)
    def _():
        seg_buf[0:8, :] = seg_buf[SPAN : SPAN + 8, :]

    seg_row = seg_ref[...].astype(F32)
    seg_buf[8 : 8 + SPAN, :] = jnp.transpose(jnp.broadcast_to(seg_row, (LANES, SPAN)))
    own = seg_buf[8 : 8 + SPAN, :]
    code = jnp.zeros((SPAN, LANES), F32)
    for step in range(1, KCONV):
        code = code + jnp.where(seg_buf[8 - step : 8 - step + SPAN, :] == own, 1.0, 0.0)
    code_ref[...] = code
    fill_conv(buf, held, b_ref, halo_ref, wb_ref, code_ref, span)
    bs_ref[...] = held[...].astype(BF16)
    latest = jnp.where(seg_row == last.astype(F32), 1.0, 0.0).astype(BF16)
    for g in range(parts):
        bt_ref[g] = jnp.transpose(bs_ref[:, g * N : (g + 1) * N]) * latest


def score_kernel(
    seg_s, c_ref, halo_ref, ids_ref, wc_ref, seg_ref, bs_ref, code_ref, token_ref,
    m_ref,
    buf, held, *, parts
):
    del token_ref
    span = pl.program_id(0)
    ids = ids_ref[...].astype(F32)
    start = span * SPAN
    before = jnp.where(span == 0, entering_id(ids, REACH - 1), seg_s[jnp.maximum(start - 1, 0)])
    fill_conv(buf, held, c_ref, halo_ref, wc_ref, code_ref, span)
    halves = [slice(half * L, (half + 1) * L) for half in range(2)]
    seg_rows = [seg_ref[:, half].astype(F32) for half in halves]
    seg_cols = [jnp.transpose(jnp.broadcast_to(seg_row, (L, L))) for seg_row in seg_rows]
    rows = lax.broadcasted_iota(jnp.int32, (L, L), 0)
    cols = lax.broadcasted_iota(jnp.int32, (L, L), 1)
    causal = rows >= cols
    across = (((1,), (1,)), ((), ()))
    for g in range(parts):
        lanes = slice(g * N, (g + 1) * N)
        cs = held[:, lanes].astype(BF16)
        early = lax.dot_general(cs, bs_ref[halves[0], lanes], across, preferred_element_type=F32)
        late = lax.dot_general(cs[L:], bs_ref[halves[1], lanes], across, preferred_element_type=F32)
        allowed = [causal & (seg_cols[half] == seg_rows[half]) for half in range(2)]
        m_ref[g, 0:L, 0:L] = jnp.where(allowed[0], early[:L], 0.0).astype(BF16)
        m_ref[g, L:SPAN, 0:L] = jnp.where(seg_cols[1] == seg_rows[0], early[L:], 0.0).astype(BF16)
        m_ref[g, 0:L, L + N :] = jnp.zeros((L, L), BF16)
        m_ref[g, L:SPAN, L + N :] = jnp.where(allowed[1], late, 0.0).astype(BF16)
        for half in range(2):
            enters = seg_cols[half] == before.astype(F32)
            m_ref[g, halves[half], L : L + N] = jnp.where(enters, held[halves[half], lanes], 0.0).astype(BF16)


def state_kernel(
    info_ref, x_ref, halo_ref, w_ref, bt_ref, a_ref, em_ref, code_ref,
    u_ref, state_ref, first_ref, factor_ref,
    buf, carry, spread, *, first_head, heads
):
    span = pl.program_id(1)
    width = x_ref.shape[1]
    chunks = width // CHUNK
    inner = CHUNK // LANES
    cut = info_ref[2 * span] > 0

    @pl.when(span == 0)
    def _():
        spread_matrix(spread, first_head + pl.program_id(0) * (width // P_SIZE), heads)
        for piece in range(width // LANES):
            buf[piece, 8 - REACH : 8, :] = halo_ref[:, piece * LANES : (piece + 1) * LANES].astype(F32)

    @pl.when(span > 0)
    def _():
        buf[:, 0:8, :] = buf[:, SPAN : SPAN + 8, :]

    def convolve(masked):
        for chunk in range(chunks):
            cols = slice(chunk * CHUNK, (chunk + 1) * CHUNK)
            scale = dot(a_ref[...], spread[:, cols])
            for piece in range(inner):
                index = chunk * inner + piece
                lanes = slice(index * LANES, (index + 1) * LANES)
                weights = 0.5 * w_ref[:, lanes].astype(F32)
                buf[index, 8 : 8 + SPAN, :] = x_ref[:, lanes].astype(F32)
                for row in range(0, SPAN, TILE):
                    code = code_ref[row : row + TILE, :] if masked else None
                    acc = conv_tile(buf, index, weights, row, TILE, code)
                    factor = scale[row : row + TILE, piece * LANES : (piece + 1) * LANES]
                    u_ref[row : row + TILE, lanes] = (silu_of_half(acc) * factor).astype(BF16)
            grown = dot(bt_ref[0], u_ref[:, cols])
            carry[span, :, cols] = grown

    @pl.when(cut)
    def _():
        convolve(True)

    @pl.when(jnp.logical_not(cut))
    def _():
        convolve(False)

    @pl.when(span == 1)
    def _():
        passes = [info_ref[2 * k + 1].astype(F32) for k in range(2)]
        for chunk in range(chunks):
            cols = slice(chunk * CHUNK, (chunk + 1) * CHUNK)
            early, late = (dot(em_ref[k], spread[:, cols])[0:1] for k in range(2))
            middle = early * carry[0, :, cols]
            first_ref[:, cols] = middle.astype(BF16)
            state_ref[:, cols] = (late * carry[1, :, cols] + (passes[1] * late * late) * middle).astype(BF16)
            factor_ref[:, cols] = (passes[0] * passes[1]) * (early * early * late * late)


def final_kernel(
    info_ref, u_ref, gate_ref, m_ref, e_ref, w_ref, em_ref, first_ref, t0_ref, t1_ref, gain_ref,
    out_ref, done_ref,
    enter, spread, held, *, first_head, heads
):
    span = pl.program_id(0)
    width = u_ref.shape[1]
    chunks = width // CHUNK
    strips = [slice(chunk * CHUNK, (chunk + 1) * CHUNK) for chunk in range(chunks)]

    @pl.when(span == 0)
    def _():
        done_ref[...] = jnp.zeros_like(done_ref)
        spread_matrix(spread, first_head, heads)
        passes = info_ref[1].astype(F32)
        for cols in strips:
            early, late = (dot(em_ref[k], spread[:, cols])[0:1] for k in range(2))
            came = t0_ref[:, cols].astype(F32) + t1_ref[:, cols].astype(F32)
            enter[0, :, cols] = (early * came).astype(BF16)
            grown = first_ref[:, cols].astype(F32) + (passes * early * early) * came
            enter[1, :, cols] = (late * grown).astype(BF16)

    squares = [jnp.zeros((L, LANES), F32) for _ in range(2)]
    for cols in strips:
        part = spread[:, cols]
        sources = jnp.concatenate([u_ref[0:L, cols], enter[span, :, cols]], axis=0)
        total = dot(m_ref[0, :, 0 : L + N], sources)
        last = dot(m_ref[0, L:SPAN, L + N :], u_ref[L:SPAN, cols])
        outer = dot(e_ref[...], part)
        direct = dot(w_ref[...], part)
        for half in range(2):
            own = slice(half * L, (half + 1) * L)
            sums = total[own] + direct[own] * u_ref[own, cols].astype(F32)
            if half == 1:
                sums = sums + last
            v = (outer[own] * sums) * silu_of_half(0.5 * gate_ref[own, cols].astype(F32))
            held[own, cols] = v
            v2 = v * v
            for piece in range(CHUNK // LANES):
                squares[half] = squares[half] + v2[:, piece * LANES : (piece + 1) * LANES]
    for half in range(2):
        own = slice(half * L, (half + 1) * L)
        mean = jnp.sum(squares[half], axis=1, keepdims=True) * (1.0 / width)
        scale = lax.rsqrt(mean + 1e-05)
        for cols in strips:
            out_ref[own, cols] = (held[own, cols] * scale * gain_ref[:, cols]).astype(BF16)


def state_after_kernel(*refs, first_head, heads):
    state_kernel(*refs[:8], *refs[9:], first_head=first_head, heads=heads)


def scale_kernel(value_ref, factor_ref, *refs):
    out_ref = refs[-1]
    for row in range(0, N, 64):
        rows = slice(row, row + 64)
        out_ref[rows] = (factor_ref[...] * value_ref[rows].astype(F32)).astype(BF16)


def final_into_kernel(*refs, first_head, heads):
    final_kernel(*refs[:11], *refs[12:], first_head=first_head, heads=heads)


def per_device(
    x_in, gate_in, b_in, c_in, dt_raw, conv_x, conv_b, conv_c, dt_bias, a_log, skip, norm_gain, segment
):
    rows, channels = x_in.shape
    width_bc = b_in.shape[1]
    parts = width_bc // N
    width = channels // parts
    heads = width // P_SIZE
    all_heads = dt_raw.shape[1]
    blocks = rows // L
    spans = rows // SPAN
    assert spans == 2
    devices = lax.axis_size("req")
    step_width = width
    shape = jax.ShapeDtypeStruct
    smem = pl.BlockSpec(memory_space=pltpu.SMEM)
    whole = lambda *_: (0, 0)
    at_row = lambda k, *_: (k, 0)

    def params(axes, mib=16):
        return pltpu.CompilerParams(dimension_semantics=("arbitrary",) * axes, vmem_limit_bytes=mib << 20)

    def cost(flops, mib):
        return pl.CostEstimate(flops=flops, bytes_accessed=mib << 20, transcendentals=0)

    x_in, b_in, c_in = (pltpu.with_memory_space_constraint(value, pltpu.HBM) for value in (x_in, b_in, c_in))
    shift = [(k, k + 1) for k in range(devices - 1)]
    inside = [(k, k + 1) for k in range(0, devices - 1, 2)]
    across = [(k, k + 1) for k in range(1, devices - 1, 2)]

    last_rows = lambda *_: (rows // 16 - 1, 0)
    tail_width = channels + 2 * width_bc + LANES
    tail = pl.pallas_call(
        tail_kernel,
        grid=(1,),
        in_specs=[
            smem,
            pl.BlockSpec((16, channels), last_rows),
            pl.BlockSpec((16, width_bc), last_rows),
            pl.BlockSpec((16, width_bc), last_rows),
        ],
        out_specs=pl.BlockSpec((REACH, tail_width), whole),
        out_shape=shape((REACH, tail_width), BF16),
        compiler_params=params(1),
        cost_estimate=cost(1000, 0),
        name="tails",
    )(segment, x_in, b_in, c_in)
    halo = lax.ppermute(tail, "req", shift)

    row = lambda value: value.reshape(1, -1)
    narrow = pl.BlockSpec((SPAN, LANES), at_row)
    a_hl, e_hl, w_hl, em = pl.pallas_call(
        decay_kernel,
        grid=(spans,),
        in_specs=[pl.BlockSpec((SPAN, all_heads), at_row)] + [pl.BlockSpec((1, all_heads), whole)] * 3,
        out_specs=[narrow, narrow, narrow, pl.BlockSpec((1, 16, LANES), lambda k: (k, 0, 0))],
        out_shape=[shape((rows, LANES), BF16)] * 3 + [shape((spans, 16, LANES), BF16)],
        compiler_params=params(1),
        cost_estimate=cost(3 * 10**9, 1),
        name="decays",
    )(dt_raw, row(dt_bias), row(a_log), row(skip))

    halo_bc = lambda which: pl.BlockSpec((REACH, width_bc), lambda *_: (0, channels // width_bc + which))
    ids_spec = pl.BlockSpec((REACH, LANES), lambda *_: (0, tail_width // LANES - 1))
    seg_spec = pl.BlockSpec((1, SPAN), lambda k: (0, k))
    wide_bc = pl.BlockSpec((SPAN, width_bc), at_row)
    conv_scratch = [pltpu.VMEM((width_bc // LANES, SPAN + 8, LANES), F32)]
    bs, bt, code, info = pl.pallas_call(
        functools.partial(b_kernel, parts=parts),
        grid=(spans,),
        in_specs=[smem, wide_bc, halo_bc(0), ids_spec, pl.BlockSpec((KCONV, width_bc), whole), seg_spec],
        out_specs=[wide_bc, pl.BlockSpec((parts, N, SPAN), lambda k: (0, 0, k)), narrow, smem],
        out_shape=[
            shape((rows, width_bc), BF16),
            shape((parts, N, rows), BF16),
            shape((rows, LANES), F32),
            shape((2 * spans,), jnp.int32),
        ],
        scratch_shapes=conv_scratch + [pltpu.VMEM((SPAN + 8, LANES), F32), pltpu.VMEM((SPAN, width_bc), F32)],
        compiler_params=params(1),
        cost_estimate=cost(10**9, 3),
        name="b_rows",
    )(segment, b_in, halo, halo, conv_b, row(segment))

    def score(token):
        return pl.pallas_call(
            functools.partial(score_kernel, parts=parts),
            grid=(spans,),
            in_specs=[
                smem, wide_bc, halo_bc(1), ids_spec, pl.BlockSpec((KCONV, width_bc), whole), seg_spec, wide_bc, narrow,
                pl.BlockSpec(memory_space=pl.ANY),
            ],
            out_specs=pl.BlockSpec((parts, SPAN, N + SPAN), lambda k: (0, k, 0)),
            out_shape=shape((parts, rows, N + SPAN), BF16),
            scratch_shapes=conv_scratch + [pltpu.VMEM((SPAN, width_bc), F32)],
            compiler_params=params(1),
            cost_estimate=cost(3 * 10**9, 4),
            name="scores",
        )(segment, c_in, halo, halo, conv_c, row(segment), bs, code, token)

    em_spec = lambda: pl.BlockSpec((spans, 16, LANES), lambda *_: (0, 0, 0))

    anywhere = pl.BlockSpec(memory_space=pl.ANY)

    def local(g, tokens):
        steps = width // step_width
        at_cols = lambda j, k: (0, g * steps + j)
        return pl.pallas_call(
            functools.partial(state_after_kernel if tokens else state_kernel, first_head=g * heads, heads=all_heads),
            grid=(steps, spans),
            in_specs=[
                smem,
                pl.BlockSpec((SPAN, step_width), lambda j, k: (k, g * steps + j)),
                pl.BlockSpec((REACH, step_width), at_cols),
                pl.BlockSpec((KCONV, step_width), at_cols),
                pl.BlockSpec((1, N, SPAN), lambda j, k: (g, 0, k)),
                pl.BlockSpec((SPAN, LANES), lambda j, k: (k, 0)),
                em_spec(),
                pl.BlockSpec((SPAN, LANES), lambda j, k: (k, 0)),
            ]
            + [anywhere] * len(tokens),
            out_specs=[
                pl.BlockSpec((SPAN, step_width), lambda j, k: (k, j)),
                pl.BlockSpec((N, step_width), lambda j, k: (0, j)),
                pl.BlockSpec((N, step_width), lambda j, k: (0, j)),
                pl.BlockSpec((1, step_width), lambda j, k: (0, j)),
            ],
            out_shape=[
                shape((rows, width), BF16),
                shape((N, width), BF16),
                shape((N, width), BF16),
                shape((1, width), F32),
            ],
            scratch_shapes=[
                pltpu.VMEM((step_width // LANES, SPAN + 8, LANES), F32),
                pltpu.VMEM((spans, N, step_width), F32),
                pltpu.VMEM((LANES, step_width), BF16),
            ],
            compiler_params=params(2, 24),
            cost_estimate=cost(6 * 10**9, 10),
            name="state",
        )(info, x_in, halo, conv_x, bt, a_hl, em, code, *tokens)

    def scaled(value, factor, token):
        tokens = [] if token is None else [token]
        whole_spec = lambda array: pl.BlockSpec(array.shape, whole)
        return pl.pallas_call(
            scale_kernel,
            grid=(1,),
            in_specs=[whole_spec(value), whole_spec(factor)] + [anywhere] * len(tokens),
            out_specs=whole_spec(value),
            out_shape=shape(value.shape, BF16),
            compiler_params=params(1),
            cost_estimate=cost(10**6, 2),
            name="scale",
        )(value, factor, *tokens)

    def leave(state, first, factor):
        return (state.astype(F32) + factor * first.astype(F32)).astype(BF16)

    def travel(state, first, leaving, factor, token):
        entering, passed = jnp.zeros_like(state), jnp.zeros_like(state)
        rounds = devices // 2 - 1
        for turn in range(rounds):
            entering = lax.ppermute(leaving, "req", across)
            passed = lax.ppermute(scaled(entering, factor, token), "req", inside[1:])
            if turn < rounds - 1:
                leaving = leave(state, first.astype(F32) + passed.astype(F32), factor)
        return first + entering, passed

    def final(g, u, m, first, carries, out):
        at_group = lambda *_: (0, g)
        own = pl.BlockSpec((SPAN, width), lambda k: (k, g))
        square = pl.BlockSpec((N, width), whole, pipeline_mode=pl.Buffered(1))
        in_specs = [
            smem,
            pl.BlockSpec((SPAN, width), at_row),
            own,
            pl.BlockSpec((1, SPAN, N + SPAN), lambda k: (g, k, 0)),
            narrow,
            narrow,
            em_spec(),
            square,
            square,
            square,
            pl.BlockSpec((1, width), at_group),
        ]
        operands = [info, u, gate_in, m, e_hl, w_hl, em, first, *carries, row(norm_gain)]
        if out is not None:
            in_specs.append(anywhere)
            operands.append(out)
        return pl.pallas_call(
            functools.partial(final_kernel if out is None else final_into_kernel, first_head=g * heads, heads=all_heads),
            grid=(spans,),
            in_specs=in_specs,
            out_specs=[own, pl.BlockSpec((8, LANES), whole)],
            out_shape=[shape((rows, channels), BF16), shape((8, LANES), F32)],
            scratch_shapes=[
                pltpu.VMEM((spans, N, width), BF16),
                pltpu.VMEM((LANES, width), BF16),
                pltpu.VMEM((SPAN, width), F32),
            ],
            input_output_aliases={} if out is None else {11: 0},
            compiler_params=params(1, 26),
            cost_estimate=cost(6 * 10**9, 16),
            name="final",
        )(*operands)

    leaving, locals_, m = None, [], None
    for g in range(parts):
        u, state, inner, factor = local(g, [leaving] if g else [])
        first = lax.ppermute(state, "req", inside)
        leaving = leave(state, first, factor)
        locals_.append((u, inner, state, first, leaving, factor))
    m = score(factor)
    out = done = None
    for g in range(parts):
        u, inner, *sent = locals_[g]
        out, done = final(g, u, m, inner, travel(*sent, m if done is None else done), out)
    return out


def solution(mesh):
    rows = P(("groups", "req"), "tp")
    placed = (rows,) * 5 + (P(None, "tp"),) * 3 + (P("tp"),) * 4 + (P(("groups", "req")),)
    return jax.shard_map(
        per_device,
        mesh=mesh,
        in_specs=placed,
        out_specs=rows,
        check_vma=False,
    )
```

```python
import functools

import jax
import jax.numpy as jnp
from jax import lax
from jax.experimental import pallas as pl
from jax.experimental.pallas import tpu as pltpu
from jax.sharding import PartitionSpec as P

P_SIZE = 64
N = 256
L = 256
SPAN = 2 * L
KCONV = 4
REACH = KCONV - 1
LANES = 128
CHUNK = 256
TILE = 128
F32 = jnp.float32
BF16 = jnp.bfloat16


def dot(a, b):
    return jnp.dot(a, b, preferred_element_type=F32)


def split_high_low(value, heads):
    lane = lax.broadcasted_iota(jnp.int32, value.shape, 1)
    high = value.astype(BF16).astype(F32)
    low = jnp.where(lane < 2 * heads, value - high, 0.0)
    return jnp.where(lane < heads, high, low).astype(BF16)


def silu_of_half(half):
    return half + half * jnp.tanh(half)


def spread_matrix(ref, first_head, heads):
    width = ref.shape[1]
    rows = lax.broadcasted_iota(jnp.int32, (LANES, width), 0) & (heads - 1)
    cols = lax.broadcasted_iota(jnp.int32, (LANES, width), 1) >> 6
    ref[...] = jnp.where(rows == cols + first_head, 1.0, 0.0).astype(BF16)


def conv_tile(buf, index, weights, row, rows, code):
    acc = None
    for step in range(KCONV):
        term = buf[index, pl.ds(8 - step + row, rows), :] * weights[REACH - step : KCONV - step]
        if code is not None and step > 0:
            term = jnp.where(code >= step, term, 0.0)
        acc = term if acc is None else acc + term
    return acc


def tail_kernel(seg_s, x_ref, b_ref, c_ref, out_ref):
    rows = seg_s.shape[0]
    start = 0
    for ref in (x_ref, b_ref, c_ref):
        width = ref.shape[1]
        value = ref[...].astype(F32)
        out_ref[:, start : start + width] = value[16 - REACH :].astype(BF16)
        start += width
    ids = [jnp.full((1, LANES), seg_s[rows - REACH + k] + 1, jnp.int32).astype(F32) for k in range(REACH)]
    out_ref[:, start:] = jnp.concatenate(ids, axis=0).astype(BF16)


def decay_kernel(dt_ref, bias_ref, a_log_ref, skip_ref, a_ref, e_ref, w_ref, em_ref):
    heads = dt_ref.shape[1]
    copies = LANES // heads
    wide = lambda value: jnp.concatenate([value] * copies, axis=1)
    z = wide(dt_ref[...].astype(F32)) + wide(bias_ref[...])
    dt = jnp.maximum(z, 0.0) + jnp.log1p(jnp.exp(-jnp.abs(z)))
    fall = -dt * wide(jnp.exp(a_log_ref[...]))
    rows = lax.broadcasted_iota(jnp.int32, (L, L), 0)
    cols = lax.broadcasted_iota(jnp.int32, (L, L), 1)
    lower = jnp.where(rows >= cols, 1.0, 0.0)
    sums = lambda value: jnp.dot(lower, value, precision=lax.Precision.HIGHEST, preferred_element_type=F32)
    upper_half = sums(fall[:L])
    cum = jnp.concatenate([upper_half, sums(fall[L:]) + upper_half[L - 1 : L]], axis=0)
    middle = 0.5 * cum[SPAN - 1 : SPAN]
    a_ref[...] = split_high_low(jnp.exp(middle - cum) * dt, heads)
    e_ref[...] = split_high_low(jnp.exp(cum - middle), heads)
    w_ref[...] = split_high_low(wide(skip_ref[...]) / dt, heads)
    em_ref[0] = split_high_low(jnp.broadcast_to(jnp.exp(middle), (16, LANES)), heads)


def fill_conv(buf, held, source, halo_ref, weights_ref, codes, span):
    pieces = source.shape[1] // LANES

    @pl.when(span == 0)
    def _():
        for piece in range(pieces):
            buf[piece, 8 - REACH : 8, :] = halo_ref[:, piece * LANES : (piece + 1) * LANES].astype(F32)

    @pl.when(span > 0)
    def _():
        for piece in range(pieces):
            buf[piece, 0:8, :] = buf[piece, SPAN : SPAN + 8, :]

    weights = 0.5 * weights_ref[...].astype(F32)
    for piece in range(pieces):
        lanes = slice(piece * LANES, (piece + 1) * LANES)
        buf[piece, 8 : 8 + SPAN, :] = source[:, lanes].astype(F32)
        for row in range(0, SPAN, TILE):
            acc = conv_tile(buf, piece, weights[:, lanes], row, TILE, codes[row : row + TILE, :])
            held[row : row + TILE, lanes] = silu_of_half(acc)


def entering_id(ids, k):
    return (jnp.max(ids[k : k + 1]) - 1.0).astype(jnp.int32)


def b_kernel(
    seg_s, b_ref, halo_ref, ids_ref, wb_ref, seg_ref,
    bs_ref, bt_ref, code_ref, info_ref,
    buf, seg_buf, held, *, parts
):
    span = pl.program_id(0)
    ids = ids_ref[...].astype(F32)
    start = span * SPAN
    first = seg_s[start]
    last = seg_s[start + SPAN - 1]
    before = jnp.where(span == 0, entering_id(ids, REACH - 1), seg_s[jnp.maximum(start - 1, 0)])
    oldest = jnp.where(span == 0, entering_id(ids, 0), seg_s[jnp.maximum(start - REACH, 0)])
    cut = (first != last) | ((oldest != first) & (oldest >= 0))
    info_ref[2 * span] = cut.astype(jnp.int32)
    info_ref[2 * span + 1] = (before == last).astype(jnp.int32)

    @pl.when(span == 0)
    def _():
        seg_buf[8 - REACH : 8, :] = ids - 1.0

    @pl.when(span > 0)
    def _():
        seg_buf[0:8, :] = seg_buf[SPAN : SPAN + 8, :]

    seg_row = seg_ref[...].astype(F32)
    seg_buf[8 : 8 + SPAN, :] = jnp.transpose(jnp.broadcast_to(seg_row, (LANES, SPAN)))
    own = seg_buf[8 : 8 + SPAN, :]
    code = jnp.zeros((SPAN, LANES), F32)
    for step in range(1, KCONV):
        code = code + jnp.where(seg_buf[8 - step : 8 - step + SPAN, :] == own, 1.0, 0.0)
    code_ref[...] = code
    fill_conv(buf, held, b_ref, halo_ref, wb_ref, code_ref, span)
    bs_ref[...] = held[...].astype(BF16)
    latest = jnp.where(seg_row == last.astype(F32), 1.0, 0.0).astype(BF16)
    for g in range(parts):
        bt_ref[g] = jnp.transpose(bs_ref[:, g * N : (g + 1) * N]) * latest


def score_kernel(
    seg_s, c_ref, halo_ref, ids_ref, wc_ref, seg_ref, bs_ref, code_ref, token_ref,
    m_ref,
    buf, held, *, parts
):
    del token_ref
    span = pl.program_id(0)
    ids = ids_ref[...].astype(F32)
    start = span * SPAN
    before = jnp.where(span == 0, entering_id(ids, REACH - 1), seg_s[jnp.maximum(start - 1, 0)])
    fill_conv(buf, held, c_ref, halo_ref, wc_ref, code_ref, span)
    halves = [slice(half * L, (half + 1) * L) for half in range(2)]
    seg_rows = [seg_ref[:, half].astype(F32) for half in halves]
    seg_cols = [jnp.transpose(jnp.broadcast_to(seg_row, (L, L))) for seg_row in seg_rows]
    rows = lax.broadcasted_iota(jnp.int32, (L, L), 0)
    cols = lax.broadcasted_iota(jnp.int32, (L, L), 1)
    causal = rows >= cols
    across = (((1,), (1,)), ((), ()))
    for g in range(parts):
        lanes = slice(g * N, (g + 1) * N)
        cs = held[:, lanes].astype(BF16)
        early = lax.dot_general(cs, bs_ref[halves[0], lanes], across, preferred_element_type=F32)
        late = lax.dot_general(cs[L:], bs_ref[halves[1], lanes], across, preferred_element_type=F32)
        allowed = [causal & (seg_cols[half] == seg_rows[half]) for half in range(2)]
        m_ref[g, 0:L, 0:L] = jnp.where(allowed[0], early[:L], 0.0).astype(BF16)
        m_ref[g, L:SPAN, 0:L] = jnp.where(seg_cols[1] == seg_rows[0], early[L:], 0.0).astype(BF16)
        m_ref[g, 0:L, L + N :] = jnp.zeros((L, L), BF16)
        m_ref[g, L:SPAN, L + N :] = jnp.where(allowed[1], late, 0.0).astype(BF16)
        for half in range(2):
            enters = seg_cols[half] == before.astype(F32)
            m_ref[g, halves[half], L : L + N] = jnp.where(enters, held[halves[half], lanes], 0.0).astype(BF16)


def state_kernel(
    info_ref, x_ref, halo_ref, w_ref, bt_ref, a_ref, em_ref, code_ref,
    u_ref, state_ref, first_ref, factor_ref,
    buf, carry, spread, *, first_head, heads
):
    span = pl.program_id(1)
    width = x_ref.shape[1]
    chunks = width // CHUNK
    inner = CHUNK // LANES
    cut = info_ref[2 * span] > 0

    @pl.when(span == 0)
    def _():
        spread_matrix(spread, first_head + pl.program_id(0) * (width // P_SIZE), heads)
        for piece in range(width // LANES):
            buf[piece, 8 - REACH : 8, :] = halo_ref[:, piece * LANES : (piece + 1) * LANES].astype(F32)

    @pl.when(span > 0)
    def _():
        buf[:, 0:8, :] = buf[:, SPAN : SPAN + 8, :]

    def convolve(masked):
        for chunk in range(chunks):
            cols = slice(chunk * CHUNK, (chunk + 1) * CHUNK)
            scale = dot(a_ref[...], spread[:, cols])
            for piece in range(inner):
                index = chunk * inner + piece
                lanes = slice(index * LANES, (index + 1) * LANES)
                weights = 0.5 * w_ref[:, lanes].astype(F32)
                buf[index, 8 : 8 + SPAN, :] = x_ref[:, lanes].astype(F32)
                for row in range(0, SPAN, TILE):
                    code = code_ref[row : row + TILE, :] if masked else None
                    acc = conv_tile(buf, index, weights, row, TILE, code)
                    factor = scale[row : row + TILE, piece * LANES : (piece + 1) * LANES]
                    u_ref[row : row + TILE, lanes] = (silu_of_half(acc) * factor).astype(BF16)
            grown = dot(bt_ref[0], u_ref[:, cols])
            carry[span, :, cols] = grown

    @pl.when(cut)
    def _():
        convolve(True)

    @pl.when(jnp.logical_not(cut))
    def _():
        convolve(False)

    @pl.when(span == 1)
    def _():
        passes = [info_ref[2 * k + 1].astype(F32) for k in range(2)]
        for chunk in range(chunks):
            cols = slice(chunk * CHUNK, (chunk + 1) * CHUNK)
            early, late = (dot(em_ref[k], spread[:, cols])[0:1] for k in range(2))
            middle = early * carry[0, :, cols]
            first_ref[:, cols] = middle.astype(BF16)
            state_ref[:, cols] = (late * carry[1, :, cols] + (passes[1] * late * late) * middle).astype(BF16)
            factor_ref[:, cols] = (passes[0] * passes[1]) * (early * early * late * late)


def final_kernel(
    info_ref, u_ref, gate_ref, m_ref, e_ref, w_ref, em_ref, first_ref, t0_ref, t1_ref, gain_ref,
    out_ref, done_ref,
    enter, spread, held, *, first_head, heads
):
    span = pl.program_id(0)
    width = u_ref.shape[1]
    chunks = width // CHUNK
    strips = [slice(chunk * CHUNK, (chunk + 1) * CHUNK) for chunk in range(chunks)]

    @pl.when(span == 0)
    def _():
        done_ref[...] = jnp.zeros_like(done_ref)
        spread_matrix(spread, first_head, heads)
        passes = info_ref[1].astype(F32)
        for cols in strips:
            early, late = (dot(em_ref[k], spread[:, cols])[0:1] for k in range(2))
            came = t0_ref[:, cols].astype(F32) + t1_ref[:, cols].astype(F32)
            enter[0, :, cols] = (early * came).astype(BF16)
            grown = first_ref[:, cols].astype(F32) + (passes * early * early) * came
            enter[1, :, cols] = (late * grown).astype(BF16)

    squares = [jnp.zeros((L, LANES), F32) for _ in range(2)]
    for cols in strips:
        part = spread[:, cols]
        sources = jnp.concatenate([u_ref[0:L, cols], enter[span, :, cols]], axis=0)
        total = dot(m_ref[0, :, 0 : L + N], sources)
        last = dot(m_ref[0, L:SPAN, L + N :], u_ref[L:SPAN, cols])
        outer = dot(e_ref[...], part)
        direct = dot(w_ref[...], part)
        for half in range(2):
            own = slice(half * L, (half + 1) * L)
            sums = total[own] + direct[own] * u_ref[own, cols].astype(F32)
            if half == 1:
                sums = sums + last
            v = (outer[own] * sums) * silu_of_half(0.5 * gate_ref[own, cols].astype(F32))
            held[own, cols] = v
            v2 = v * v
            for piece in range(CHUNK // LANES):
                squares[half] = squares[half] + v2[:, piece * LANES : (piece + 1) * LANES]
    for half in range(2):
        own = slice(half * L, (half + 1) * L)
        mean = jnp.sum(squares[half], axis=1, keepdims=True) * (1.0 / width)
        scale = lax.rsqrt(mean + 1e-05)
        for cols in strips:
            out_ref[own, cols] = (held[own, cols] * scale * gain_ref[:, cols]).astype(BF16)


def state_after_kernel(*refs, first_head, heads):
    state_kernel(*refs[:8], *refs[9:], first_head=first_head, heads=heads)


def scale_kernel(value_ref, factor_ref, *refs):
    out_ref = refs[-1]
    for row in range(0, N, 64):
        rows = slice(row, row + 64)
        out_ref[rows] = (factor_ref[...] * value_ref[rows].astype(F32)).astype(BF16)


def final_into_kernel(*refs, first_head, heads):
    final_kernel(*refs[:11], *refs[12:], first_head=first_head, heads=heads)


def per_device(
    x_in, gate_in, b_in, c_in, dt_raw, conv_x, conv_b, conv_c, dt_bias, a_log, skip, norm_gain, segment
):
    rows, channels = x_in.shape
    width_bc = b_in.shape[1]
    parts = width_bc // N
    width = channels // parts
    heads = width // P_SIZE
    all_heads = dt_raw.shape[1]
    blocks = rows // L
    spans = rows // SPAN
    assert spans == 2
    devices = lax.axis_size("req")
    step_width = width
    shape = jax.ShapeDtypeStruct
    smem = pl.BlockSpec(memory_space=pltpu.SMEM)
    whole = lambda *_: (0, 0)
    at_row = lambda k, *_: (k, 0)

    def params(axes, mib=16):
        return pltpu.CompilerParams(dimension_semantics=("arbitrary",) * axes, vmem_limit_bytes=mib << 20)

    def cost(flops, mib):
        return pl.CostEstimate(flops=flops, bytes_accessed=mib << 20, transcendentals=0)

    x_in, b_in, c_in = (pltpu.with_memory_space_constraint(value, pltpu.HBM) for value in (x_in, b_in, c_in))
    shift = [(k, k + 1) for k in range(devices - 1)]
    inside = [(k, k + 1) for k in range(0, devices - 1, 2)]
    across = [(k, k + 1) for k in range(1, devices - 1, 2)]

    last_rows = lambda *_: (rows // 16 - 1, 0)
    tail_width = channels + 2 * width_bc + LANES
    tail = pl.pallas_call(
        tail_kernel,
        grid=(1,),
        in_specs=[
            smem,
            pl.BlockSpec((16, channels), last_rows),
            pl.BlockSpec((16, width_bc), last_rows),
            pl.BlockSpec((16, width_bc), last_rows),
        ],
        out_specs=pl.BlockSpec((REACH, tail_width), whole),
        out_shape=shape((REACH, tail_width), BF16),
        compiler_params=params(1),
        cost_estimate=cost(1000, 0),
        name="tails",
    )(pltpu.with_memory_space_constraint(segment, pltpu.HBM), x_in, b_in, c_in)
    halo = lax.ppermute(tail, "req", shift)

    row = lambda value: value.reshape(1, -1)
    narrow = pl.BlockSpec((SPAN, LANES), at_row)
    a_hl, e_hl, w_hl, em = pl.pallas_call(
        decay_kernel,
        grid=(spans,),
        in_specs=[pl.BlockSpec((SPAN, all_heads), at_row)] + [pl.BlockSpec((1, all_heads), whole)] * 3,
        out_specs=[narrow, narrow, narrow, pl.BlockSpec((1, 16, LANES), lambda k: (k, 0, 0))],
        out_shape=[shape((rows, LANES), BF16)] * 3 + [shape((spans, 16, LANES), BF16)],
        compiler_params=params(1),
        cost_estimate=cost(3 * 10**9, 1),
        name="decays",
    )(dt_raw, row(dt_bias), row(a_log), row(skip))

    halo_bc = lambda which: pl.BlockSpec((REACH, width_bc), lambda *_: (0, channels // width_bc + which))
    ids_spec = pl.BlockSpec((REACH, LANES), lambda *_: (0, tail_width // LANES - 1))
    seg_spec = pl.BlockSpec((1, SPAN), lambda k: (0, k))
    wide_bc = pl.BlockSpec((SPAN, width_bc), at_row)
    conv_scratch = [pltpu.VMEM((width_bc // LANES, SPAN + 8, LANES), F32)]
    bs, bt, code, info = pl.pallas_call(
        functools.partial(b_kernel, parts=parts),
        grid=(spans,),
        in_specs=[smem, wide_bc, halo_bc(0), ids_spec, pl.BlockSpec((KCONV, width_bc), whole), seg_spec],
        out_specs=[wide_bc, pl.BlockSpec((parts, N, SPAN), lambda k: (0, 0, k)), narrow, smem],
        out_shape=[
            shape((rows, width_bc), BF16),
            shape((parts, N, rows), BF16),
            shape((rows, LANES), F32),
            shape((2 * spans,), jnp.int32),
        ],
        scratch_shapes=conv_scratch + [pltpu.VMEM((SPAN + 8, LANES), F32), pltpu.VMEM((SPAN, width_bc), F32)],
        compiler_params=params(1),
        cost_estimate=cost(10**9, 3),
        name="b_rows",
    )(segment, b_in, halo, halo, conv_b, row(segment))

    def score(token):
        return pl.pallas_call(
            functools.partial(score_kernel, parts=parts),
            grid=(spans,),
            in_specs=[
                smem, wide_bc, halo_bc(1), ids_spec, pl.BlockSpec((KCONV, width_bc), whole), seg_spec, wide_bc, narrow,
                pl.BlockSpec(memory_space=pl.ANY),
            ],
            out_specs=pl.BlockSpec((parts, SPAN, N + SPAN), lambda k: (0, k, 0)),
            out_shape=shape((parts, rows, N + SPAN), BF16),
            scratch_shapes=conv_scratch + [pltpu.VMEM((SPAN, width_bc), F32)],
            compiler_params=params(1),
            cost_estimate=cost(3 * 10**9, 4),
            name="scores",
        )(segment, c_in, halo, halo, conv_c, row(segment), bs, code, token)

    em_spec = lambda: pl.BlockSpec((spans, 16, LANES), lambda *_: (0, 0, 0))

    anywhere = pl.BlockSpec(memory_space=pl.ANY)

    def local(g, tokens):
        steps = width // step_width
        at_cols = lambda j, k: (0, g * steps + j)
        return pl.pallas_call(
            functools.partial(state_after_kernel if tokens else state_kernel, first_head=g * heads, heads=all_heads),
            grid=(steps, spans),
            in_specs=[
                smem,
                pl.BlockSpec((SPAN, step_width), lambda j, k: (k, g * steps + j)),
                pl.BlockSpec((REACH, step_width), at_cols),
                pl.BlockSpec((KCONV, step_width), at_cols),
                pl.BlockSpec((1, N, SPAN), lambda j, k: (g, 0, k)),
                pl.BlockSpec((SPAN, LANES), lambda j, k: (k, 0)),
                em_spec(),
                pl.BlockSpec((SPAN, LANES), lambda j, k: (k, 0)),
            ]
            + [anywhere] * len(tokens),
            out_specs=[
                pl.BlockSpec((SPAN, step_width), lambda j, k: (k, j)),
                pl.BlockSpec((N, step_width), lambda j, k: (0, j)),
                pl.BlockSpec((N, step_width), lambda j, k: (0, j)),
                pl.BlockSpec((1, step_width), lambda j, k: (0, j)),
            ],
            out_shape=[
                shape((rows, width), BF16),
                shape((N, width), BF16),
                shape((N, width), BF16),
                shape((1, width), F32),
            ],
            scratch_shapes=[
                pltpu.VMEM((step_width // LANES, SPAN + 8, LANES), F32),
                pltpu.VMEM((spans, N, step_width), F32),
                pltpu.VMEM((LANES, step_width), BF16),
            ],
            compiler_params=params(2, 24),
            cost_estimate=cost(6 * 10**9, 10),
            name="state",
        )(info, x_in, halo, conv_x, bt, a_hl, em, code, *tokens)

    def scaled(value, factor, token):
        tokens = [] if token is None else [token]
        whole_spec = lambda array: pl.BlockSpec(array.shape, whole)
        return pl.pallas_call(
            scale_kernel,
            grid=(1,),
            in_specs=[whole_spec(value), whole_spec(factor)] + [anywhere] * len(tokens),
            out_specs=whole_spec(value),
            out_shape=shape(value.shape, BF16),
            compiler_params=params(1),
            cost_estimate=cost(10**6, 2),
            name="scale",
        )(value, factor, *tokens)

    def leave(state, first, factor):
        return (state.astype(F32) + factor * first.astype(F32)).astype(BF16)

    def travel(state, first, leaving, factor, token):
        entering, passed = jnp.zeros_like(state), jnp.zeros_like(state)
        rounds = devices // 2 - 1
        for turn in range(rounds):
            entering = lax.ppermute(leaving, "req", across)
            passed = lax.ppermute(scaled(entering, factor, token), "req", inside[1:])
            if turn < rounds - 1:
                leaving = leave(state, first.astype(F32) + passed.astype(F32), factor)
        return first + entering, passed

    def final(g, u, m, first, carries, out):
        at_group = lambda *_: (0, g)
        own = pl.BlockSpec((SPAN, width), lambda k: (k, g))
        square = pl.BlockSpec((N, width), whole, pipeline_mode=pl.Buffered(1))
        in_specs = [
            smem,
            pl.BlockSpec((SPAN, width), at_row),
            own,
            pl.BlockSpec((1, SPAN, N + SPAN), lambda k: (g, k, 0)),
            narrow,
            narrow,
            em_spec(),
            square,
            square,
            square,
            pl.BlockSpec((1, width), at_group),
        ]
        operands = [info, u, gate_in, m, e_hl, w_hl, em, first, *carries, row(norm_gain)]
        if out is not None:
            in_specs.append(anywhere)
            operands.append(out)
        return pl.pallas_call(
            functools.partial(final_kernel if out is None else final_into_kernel, first_head=g * heads, heads=all_heads),
            grid=(spans,),
            in_specs=in_specs,
            out_specs=[own, pl.BlockSpec((8, LANES), whole)],
            out_shape=[shape((rows, channels), BF16), shape((8, LANES), F32)],
            scratch_shapes=[
                pltpu.VMEM((spans, N, width), BF16),
                pltpu.VMEM((LANES, width), BF16),
                pltpu.VMEM((SPAN, width), F32),
            ],
            input_output_aliases={} if out is None else {11: 0},
            compiler_params=params(1, 26),
            cost_estimate=cost(6 * 10**9, 16),
            name="final",
        )(*operands)

    leaving, locals_, m = None, [], None
    for g in range(parts):
        u, state, inner, factor = local(g, [leaving] if g else [])
        first = lax.ppermute(state, "req", inside)
        leaving = leave(state, first, factor)
        locals_.append((u, inner, state, first, leaving, factor))
    m = score(factor)
    out = done = None
    for g in range(parts):
        u, inner, *sent = locals_[g]
        out, done = final(g, u, m, inner, travel(*sent, m if done is None else done), out)
    return out


def solution(mesh):
    rows = P(("groups", "req"), "tp")
    placed = (rows,) * 5 + (P(None, "tp"),) * 3 + (P("tp"),) * 4 + (P(("groups", "req")),)
    return jax.shard_map(
        per_device,
        mesh=mesh,
        in_specs=placed,
        out_specs=rows,
        check_vma=False,
    )
```
